512 devices in a mesh: seg: 64 (over z, x_hi, core), space: 8 (over x_lo, y).
Axes of the slice: x: 4 (x_hi: 2, x_lo: 2; x = x_hi * 2 + x_lo), y: 4, z: 16, core: 2. Of those that a mesh axis runs over, the one named last changes fastest.
Arguments:
- states: float32 [64, 3, 64, 2560], P('seg', None, 'space'), may hold values from -5.25 to 5.25
- tangent_panel: float32 [64, 2, 3, 64, 2560], P('seg', None, None, 'space'), may hold values from -9.3 to 9.3
- wall_inverse: float32 [64, 40, 40], P('space'), may hold values from -0.25 to 0.95
- keep_mask: int32 [64, 64], replicated, may hold values 0 or 1
Outputs:
- corrected: float32 [64, 3, 64, 2560], P('seg', None, 'space')
- new_residual: float32 [64, 3, 64, 2560], P('seg', None, 'space')
The draws below stay inside these ranges and needn't reach their ends.
All inputs are finite; a program needn't handle non-finite values.
Results may differ from the reference program's by a relative error of at most 0.0004.
Values sent between devices are 32-bit elements; how exact they have to be, the bound alone decides.
A program may use at most 64 MiB of HBM per device.

```python
import math
import jax
import jax.numpy as jnp
from jax import lax

NX = 64
NY = 40
NZ = 64
STEPS = 1
NSEG = 64


def wall_profile():
    indices = jnp.arange(1, NY + 1, dtype=jnp.int32)
    heights = jnp.cos(math.pi / (NY + 1) * indices.astype(jnp.float32))
    return 1.0 - heights * heights


def flat_profile():
    return jnp.broadcast_to(wall_profile()[:, None], (NY, NZ)).reshape(NY * NZ)


def shared_field(key):
    values = jnp.clip(jax.random.normal(key, (NSEG, 3, NX, NY * NZ), jnp.float32), -6.0, 6.0)
    return flat_profile() * values


def draw_states(key, part):
    common = shared_field(key)
    key = jax.random.fold_in(key, 11)
    rough = jax.random.uniform(key, common.shape, jnp.float32, 0.5, 1.5)
    return 0.5 * common * rough


def draw_tangent_panel(key, part):
    common = shared_field(key)
    key = jax.random.fold_in(key, 23)
    noise = jnp.clip(jax.random.normal(key, (NSEG, 2, 3, NX, NY * NZ), jnp.float32), -6.0, 6.0)
    noise = flat_profile() * noise
    leading = 0.6 * common + 0.8 * noise[:, 0]
    return jnp.stack([leading, 0.5 * leading + 0.85 * noise[:, 1]], axis=1)


def draw_wall_inverse(key, part):
    key = jax.random.fold_in(key, 37)
    diag_key, cross_key = jax.random.split(key)
    identity = (jnp.arange(NY)[:, None] == jnp.arange(NY)[None, :]).astype(jnp.float32)
    diagonal = jax.random.uniform(diag_key, (NX, NY, 1), jnp.float32, 0.55, 0.95)
    crossing = jnp.clip(jax.random.normal(cross_key, (NX, NY, NY), jnp.float32), -4.0, 4.0)
    row_weight = wall_profile()[None, :, None]
    return identity * diagonal + (1.0 - identity) * (0.25 / math.sqrt(NY)) * row_weight * crossing


def touch_ends(values, own_key, least, largest):
    longest = values.shape.index(max(values.shape))
    spots = []
    for shift in (0, 1):
        where = [jax.random.randint(jax.random.fold_in(own_key, axis), (), 0, length) for axis, length in enumerate(values.shape)]
        where[longest] = (where[longest] + shift) % values.shape[longest]
        spots.append(tuple(where))
    return values.at[spots[0]].set(least).at[spots[1]].set(largest)


def setup_inputs(seed: int = 0) -> dict:
    keys = jax.random.split(jax.random.key(seed), 5)
    return {
        "states": draw_states(jax.random.fold_in(keys[4], 71), 0),
        "tangent_panel": draw_tangent_panel(jax.random.fold_in(keys[4], 71), 0),
        "wall_inverse": draw_wall_inverse(jax.random.fold_in(keys[4], 71), 0),
        "keep_mask": touch_ends((jax.random.randint(keys[3], (NX, NZ), 0, 4) < 3).astype(jnp.int32), jax.random.fold_in(keys[3], 1), 0, 1),
    }


TIME_STEP = 0.005
VISCOSITY = 0.0025
STREAM_WAVE = 1.0
SPAN_WAVE = 2.0
PRECISE = lax.Precision.HIGHEST

def fourier_basis(length, stretch):
    indices = jnp.arange(length, dtype=jnp.int32)
    mode_row = indices[:, None]
    point_col = indices[None, :]
    wavenumber = jnp.where(mode_row == length - 1, length // 2, (mode_row + 1) // 2)
    phases = 2.0 * math.pi / length * (wavenumber * point_col % length).astype(jnp.float32)
    boundary = (mode_row == 0) | (mode_row == length - 1)
    amplitude = jnp.where(boundary, math.sqrt(1.0 / length), math.sqrt(2.0 / length))
    is_cosine = (mode_row % 2 == 1) | (mode_row == 0)
    basis_rows = amplitude * jnp.where(is_cosine, jnp.cos(phases), jnp.sin(phases))
    slope_rows = stretch * wavenumber.astype(jnp.float32) * amplitude * jnp.where(is_cosine, -jnp.sin(phases), jnp.cos(phases))
    slope_rows = jnp.where(boundary, jnp.zeros_like(slope_rows), slope_rows)
    return (basis_rows, slope_rows)

def wall_tables(length):
    indices = jnp.arange(1, length + 1, dtype=jnp.int32)
    heights = jnp.cos(math.pi / (length + 1) * indices.astype(jnp.float32))
    row_height = heights[:, None]
    col_height = heights[None, :]
    parity = jnp.where((indices[:, None] + indices[None, :]) % 2 == 0, 1.0, -1.0)
    diagonal_mask = indices[:, None] == indices[None, :]
    spacing = jnp.where(diagonal_mask, 1.0, row_height - col_height)
    derivative = jnp.where(diagonal_mask, -row_height / (2.0 * (1.0 - row_height * row_height)), parity / spacing)
    return (heights, derivative)

def span_damping(length):
    indices = jnp.arange(length, dtype=jnp.int32)
    wavenumber = jnp.where(indices == length - 1, length // 2, (indices + 1) // 2).astype(jnp.float32)
    return 1.0 / (1.0 + TIME_STEP * VISCOSITY * (SPAN_WAVE * wavenumber) ** 2)

def along_z(values, matrix):
    return jnp.einsum('fmyk,kz->fmyz', values, matrix, precision=PRECISE)

def along_x(values, matrix):
    return jnp.einsum('fmyz,mx->fxyz', values, matrix, precision=PRECISE)

def along_y(values, matrix):
    return jnp.einsum('ij,fmjk->fmik', matrix, values, precision=PRECISE)

def regroup(values):
    return values.reshape((3, 3) + values.shape[1:])

def forcing(physical, stream_slope, wall_slope, span_slope, heights):
    current = physical[0]
    velocity = heights[None, :, None] + current[0]
    carried = velocity[None, None] * stream_slope + current[1][None, None] * wall_slope + current[2][None, None] * span_slope
    pushed = physical[:, 0:1] * stream_slope[0][None] + physical[:, 1:2] * wall_slope[0][None] + physical[:, 2:3] * span_slope[0][None]
    selector = (jnp.arange(3, dtype=jnp.int32) > 0).astype(physical.dtype)[:, None, None, None, None]
    tendency = -(carried + selector * pushed)
    return tendency.at[:, 0].add(-physical[:, 1])

def advance(fields, inverse, kept_modes, damping, tables):
    stream_basis, stream_deriv, span_basis, span_deriv, heights, wall_deriv = tables
    for repeat in range(STEPS):
        wall_part = along_y(fields, wall_deriv)
        span_part = along_z(fields, span_basis)
        physical = along_x(span_part, stream_basis)
        stream_slope = along_x(span_part, stream_deriv)
        span_slope = along_x(along_z(fields, span_deriv), stream_basis)
        wall_slope = along_x(along_z(wall_part, span_basis), stream_basis)
        tendency = forcing(regroup(physical), regroup(stream_slope), regroup(wall_slope), regroup(span_slope), heights)
        spectral = along_x(along_z(tendency.reshape(physical.shape), span_basis.T), stream_basis.T)
        forced = kept_modes * (fields + TIME_STEP * spectral)
        fields = damping * jnp.einsum('myj,fmjk->fmyk', inverse, forced, precision=PRECISE)
    return fields

def reference(states, tangent_panel, wall_inverse, keep_mask):
    stream_count = keep_mask.shape[0]
    span_count = keep_mask.shape[1]
    wall_count = wall_inverse.shape[1]
    stream_basis, stream_deriv = fourier_basis(stream_count, STREAM_WAVE)
    span_basis, span_deriv = fourier_basis(span_count, SPAN_WAVE)
    heights, wall_deriv = wall_tables(wall_count)
    tables = (stream_basis, stream_deriv, span_basis, span_deriv, heights, wall_deriv)
    kept_modes = keep_mask.astype(jnp.float32)[:, None, :]
    damping = span_damping(span_count)

    def advance_segment(inputs):
        start_state, columns = inputs
        fields = jnp.concatenate([start_state[None], columns], axis=0).reshape(9, stream_count, wall_count, span_count)
        result = advance(fields, wall_inverse, kept_modes, damping, tables)
        return result.reshape(3, 3, stream_count, wall_count * span_count)
    ends = lax.map(advance_segment, (states, tangent_panel))
    finish = ends[:, 0]
    image_end = ends[:, 1:]
    residual = finish - jnp.roll(states, -1, axis=0)
    image = image_end - jnp.roll(tangent_panel, -1, axis=0)
    drift = finish - states
    count = states.size
    summed = (0, 2, 3, 4)
    border = lax.optimization_barrier(jnp.sum(drift[:, None] * tangent_panel, axis=summed)) / math.sqrt(count)
    diag = lax.optimization_barrier(jnp.sum(image * image, axis=summed)) + border * border
    first = -lax.optimization_barrier(jnp.sum(image * residual[:, None], axis=summed)) / diag
    moved = residual + jnp.einsum('k,skcxy->scxy', first, image, precision=PRECISE)
    lift = jnp.sum(border * first)
    second = -(lax.optimization_barrier(jnp.sum(image * moved[:, None], axis=summed)) + border * lift) / diag
    new_residual = moved + jnp.einsum('k,skcxy->scxy', second, image, precision=PRECISE)
    corrected = states + jnp.einsum('k,skcxy->scxy', first + second, tangent_panel, precision=PRECISE)
    return (corrected, new_residual)
```

```python
import functools
import math

import jax
import jax.numpy as jnp
import ml_dtypes
import numpy as np
from jax import lax
from jax.experimental import pallas as pl
from jax.experimental.pallas import tpu as pltpu
from jax.sharding import PartitionSpec as P

TIME_STEP = 0.005
VISCOSITY = 0.0025
STREAM_WAVE = 1.0
SPAN_WAVE = 2.0
MESH = pl.DeviceIdType.MESH
NX, NY, NZ = 64, 40, 64
TILE = 128
PAIRS = NY // 2
LANES = NY * NZ


def fourier_basis(length, stretch):
    mode = np.arange(length)[:, None]
    point = np.arange(length)[None, :]
    wave = np.where(mode == length - 1, length // 2, (mode + 1) // 2)
    phase = 2.0 * math.pi / length * (wave * point % length)
    edge = (mode == 0) | (mode == length - 1)
    amplitude = np.where(edge, math.sqrt(1.0 / length), math.sqrt(2.0 / length))
    cosine = (mode % 2 == 1) | (mode == 0)
    basis = amplitude * np.where(cosine, np.cos(phase), np.sin(phase))
    slope = stretch * wave * amplitude * np.where(cosine, -np.sin(phase), np.cos(phase))
    return basis, np.where(edge, 0.0, slope)


def wall_tables(length):
    index = np.arange(1, length + 1)
    height = np.cos(math.pi / (length + 1) * index)
    row, col = height[:, None], height[None, :]
    parity = np.where((index[:, None] + index[None, :]) % 2 == 0, 1.0, -1.0)
    same = index[:, None] == index[None, :]
    spacing = np.where(same, 1.0, row - col)
    return height, np.where(same, -row / (2.0 * (1.0 - row * row)), parity / spacing)


def span_damping(length):
    index = np.arange(length)
    wave = np.where(index == length - 1, length // 2, (index + 1) // 2)
    return 1.0 / (1.0 + TIME_STEP * VISCOSITY * (SPAN_WAVE * wave) ** 2)


def parts(matrix):
    high = matrix.astype(np.float32).astype(ml_dtypes.bfloat16)
    low = (matrix - high.astype(np.float64)).astype(np.float32).astype(ml_dtypes.bfloat16)
    return high, low


def twice(matrix):
    zero = np.zeros_like(matrix)
    return np.block([[matrix, zero], [zero, matrix]])


def tables():
    qx, sx = fourier_basis(NX, STREAM_WAVE)
    qz, sz = fourier_basis(NZ, SPAN_WAVE)
    height, wall = wall_tables(NY)
    high, low = parts(np.concatenate([qx.T, sx.T], axis=0))
    x_forward = np.concatenate([high, high, low], axis=1)
    high, low = parts(qx)
    x_back = np.concatenate([high, high, low], axis=1)
    high, low = parts(np.concatenate([twice(qz), twice(sz)], axis=1))
    z_forward = np.concatenate([high, high, low], axis=0)
    high, low = parts(-TIME_STEP * twice(qz.T))
    z_back = np.concatenate([high, high, low], axis=0)
    derivative = np.zeros((PAIRS, 2 * PAIRS, TILE))
    for half in (0, 1):
        lanes = slice(half * NZ, (half + 1) * NZ)
        derivative[:, 0::2, lanes] = wall[half::2, half::2][:, :, None]
        derivative[:, 1::2, lanes] = wall[half::2, 1 - half :: 2][:, :, None]
    heights = np.repeat(height.reshape(PAIRS, 1, 2), NZ, axis=2)
    damping = np.tile(span_damping(NZ), 2)[None, :]
    single = [value.astype(np.float32) for value in (derivative, heights, damping)]
    return (x_forward, x_back, z_forward, z_back, *single)


def band(place):
    row, side = lax.rem(place, 4), lax.div(place, 4)
    odd = lax.rem(row, 2)
    count = 3 - lax.rem(row + side, 2)
    return 5 * row + side * (3 - odd), count


def tile_at(index, tiles=1):
    return pl.ds(pl.multiple_of(index * TILE, TILE), tiles * TILE)


def split(value):
    high = value.astype(jnp.bfloat16)
    low = (value - high.astype(jnp.float32)).astype(jnp.bfloat16)
    return high, low


def stacked(value, axis):
    high, low = split(value)
    return jnp.concatenate([high, low, high], axis=axis)


def mul(a, b):
    return jnp.dot(a, b, preferred_element_type=jnp.float32)


def kernel(
    nseg,
    states,
    panel,
    wall,
    mask,
    x_forward_in,
    x_back_in,
    z_forward_in,
    z_back_in,
    derivative_in,
    heights_in,
    damping_in,
    corrected,
    new_residual,
    x_forward,
    x_back,
    z_forward,
    z_back,
    derivative,
    heights,
    damping,
    wall_v,
    mask_v,
    fields,
    swapped,
    slopes,
    got,
    flow,
    outgoing,
    returned,
    solve,
    forced,
    turned,
    ends,
    later,
    near,
    far,
    in_sem,
    out_send,
    out_recv,
    back_send,
    back_recv,
    later_send,
    later_recv,
    sum_send,
    sum_recv,
):
    seg = lax.axis_index("seg")
    place = lax.axis_index("space")
    core = lax.rem(seg, 2)
    chip_pair = lax.div(seg, 2)
    before = lax.rem(seg + nseg - 1, nseg)
    across = lax.rem(seg + nseg + 2 * core - 1, nseg)
    near_count, far_count = 16, nseg // 2
    near_me = core * 8 + place
    first_pair, count = band(place)

    def near_device(step):
        other = lax.rem(near_me + step, near_count)
        return (seg - core + lax.div(other, 8), lax.rem(other, 8))

    def far_device(step):
        return (2 * lax.rem(chip_pair + step, far_count) + core, place)

    barrier = pltpu.get_barrier_semaphore()
    for step in range(1, near_count):
        pl.semaphore_signal(barrier, inc=1, device_id=near_device(step), device_id_type=MESH)
    pl.semaphore_signal(barrier, inc=1, device_id=(across, place), device_id_type=MESH)
    for step in range(1, far_count):
        pl.semaphore_signal(barrier, inc=1, device_id=far_device(step), device_id_type=MESH)

    loads = [
        (states.at[0], fields.at[pl.ds(0, 3)]),
        (panel.at[0, 0], fields.at[pl.ds(3, 3)]),
        (panel.at[0, 1], fields.at[pl.ds(6, 3)]),
        (derivative_in, derivative),
        (wall, wall_v),
        (mask, mask_v),
        (x_forward_in, x_forward),
        (z_forward_in, z_forward),
        (x_back_in, x_back),
        (z_back_in, z_back),
        (heights_in, heights),
        (damping_in, damping),
    ]
    loads = [
        pltpu.make_async_copy(src, dst, in_sem.at[index])
        for index, (src, dst) in enumerate(loads)
    ]
    for load in loads:
        load.start()
    pl.semaphore_wait(barrier, near_count + far_count - 1)

    def send_heights(unit, group, source):
        for step in range(1, 8):
            other = lax.rem(place + step, 8)
            other_first, other_count = band(other)
            pltpu.make_async_remote_copy(
                src_ref=source.at[:, :, tile_at(other_first, 2)],
                dst_ref=got.at[unit, group, :, place, :, pl.ds(0, 2 * TILE)],
                send_sem=out_send.at[unit, group],
                recv_sem=out_recv.at[unit, group],
                device_id=(seg, other),
                device_id_type=MESH,
            ).start()

            @pl.when(other_count == 3)
            def _():
                pltpu.make_async_remote_copy(
                    src_ref=source.at[:, :, tile_at(other_first + 2)],
                    dst_ref=got.at[unit, group, :, place, :, pl.ds(2 * TILE, TILE)],
                    send_sem=out_send.at[unit, group],
                    recv_sem=out_recv.at[unit, group],
                    device_id=(seg, other),
                    device_id_type=MESH,
                ).start()

    def keep_heights(unit, group, source):
        got[unit, group, :, place, :, pl.ds(0, 2 * TILE)] = source[
            pl.ds(3 * group, 3), :, tile_at(first_pair, 2)
        ]

        @pl.when(count == 3)
        def _():
            got[unit, group, :, place, :, pl.ds(2 * TILE, TILE)] = source[
                pl.ds(3 * group, 3), :, tile_at(first_pair + 2)
            ]

    def drain(ref, sem):
        pltpu.make_async_copy(ref, ref, sem).wait()

    def wait_heights(unit, group):
        @pl.when(count == 3)
        def _():
            drain(
                got.at[unit, group, :, pl.ds(0, 7), :, pl.ds(0, 3 * TILE)],
                out_recv.at[unit, group],
            )

        @pl.when(count == 2)
        def _():
            drain(
                got.at[unit, group, :, pl.ds(0, 7), :, pl.ds(0, 2 * TILE)],
                out_recv.at[unit, group],
            )

    def wait_pairs(sem):
        @pl.when(count == 3)
        def _():
            drain(returned.at[0, :, :, pl.ds(0, (PAIRS - 3) * TILE)], sem)

        @pl.when(count == 2)
        def _():
            drain(returned.at[0, :, :, pl.ds(0, (PAIRS - 2) * TILE)], sem)

    def across_heights(group, source, other, coefficient, target):
        rows = pl.ds(3 * group, 3)

        def step(index, carry):
            sums = [jnp.zeros((3, 8, TILE), jnp.float32) for _ in range(2)]
            for pair in range(PAIRS):
                lanes = pl.ds(pair * TILE, TILE)
                straight, turned_pair = source[rows, :, lanes], other[rows, :, lanes]
                for which in range(2):
                    sums[which] += coefficient(2 * index + which, 2 * pair) * straight
                    sums[which] += coefficient(2 * index + which, 2 * pair + 1) * turned_pair
            target[rows, :, tile_at(2 * index)] = sums[0]
            target[rows, :, tile_at(2 * index + 1)] = sums[1]
            return carry

        lax.fori_loop(0, PAIRS // 2, step, 0)

    def turn(group, source, target):
        rows = pl.ds(3 * group, 3)
        for pair in range(PAIRS):
            lanes = pl.ds(pair * TILE, TILE)
            target[rows, :, lanes] = pltpu.roll(source[rows, :, lanes], NZ, 2)

    for group in range(3):
        source = states.at[0] if group == 0 else panel.at[0, group - 1]
        send_heights(0, group, source)
        loads[group].wait()
        if group == 0:
            loads[3].wait()
        turn(group, fields, swapped)
        across_heights(
            group,
            fields,
            swapped,
            lambda pair, row: derivative[pair, pl.ds(row, 1), :],
            slopes,
        )
        send_heights(1, group, slopes.at[pl.ds(3 * group, 3)])
        keep_heights(0, group, fields)
        keep_heights(1, group, slopes)

    shift = [
        pltpu.make_async_remote_copy(
            src_ref=src,
            dst_ref=dst,
            send_sem=later_send.at[index],
            recv_sem=later_recv.at[index],
            device_id=(before, place),
            device_id_type=MESH,
        )
        for index, (src, dst) in enumerate(
            [
                (states.at[0], later.at[pl.ds(0, 3)]),
                (panel.at[0, 0], later.at[pl.ds(3, 3)]),
                (panel.at[0, 1], later.at[pl.ds(6, 3)]),
            ]
        )
    ]
    for copy in shift:
        copy.start()
    for load in loads[4:]:
        load.wait()

    lane = lax.broadcasted_iota(jnp.int32, (8, TILE), 1)
    low_half = lane < NZ

    def solve_rows(pair, carry):
        even = wall_v[pl.ds(2 * pair, 8, stride=NY), :]
        odd = wall_v[pl.ds(2 * pair + 1, 8, stride=NY), :]

        def spread(value, column):
            return jnp.broadcast_to(value[:, column : column + 1], (8, TILE))

        for other in range(PAIRS):
            solve[pair, 2 * other] = jnp.where(
                low_half, spread(even, 2 * other), spread(odd, 2 * other + 1)
            )
            solve[pair, 2 * other + 1] = jnp.where(
                low_half, spread(even, 2 * other + 1), spread(odd, 2 * other)
            )
        return carry

    lax.fori_loop(0, PAIRS, solve_rows, 0)

    own_rows = mask_v[pl.ds(pl.multiple_of(place * 8, 8), 8), :].astype(jnp.float32)
    keep = jnp.concatenate([own_rows, own_rows], axis=1) * damping[...]

    def transform(group):
        def step(index, carry):
            lanes = tile_at(index)

            def modes(unit):
                value = got[unit, group, :, :, :, lanes]
                value = value.reshape(3, NX, TILE)
                return stacked(jnp.concatenate([value[0], value[1], value[2]], axis=1), 0)

            def by_rows(value):
                return [value[:, c * TILE : (c + 1) * TILE] for c in range(3)]

            in_x = mul(x_forward[...], modes(0))
            in_x_wall = mul(x_forward[pl.ds(0, NX), :], modes(1))
            plain = jnp.concatenate(by_rows(in_x[:NX]), axis=0)
            rest = jnp.concatenate(by_rows(in_x[NX:]) + by_rows(in_x_wall), axis=0)
            pair = mul(stacked(plain, 1), z_forward[...])
            single = mul(stacked(rest, 1), z_forward[:, pl.ds(0, TILE)])

            def field(value, c):
                return value[c * NX : (c + 1) * NX]

            physical = [field(pair[:, :TILE], c) for c in range(3)]
            span = [field(pair[:, TILE:], c) for c in range(3)]
            stream = [field(single, c) for c in range(3)]
            slope = [field(single, c + 3) for c in range(3)]
            if group == 0:
                for c in range(3):
                    flow[index, c] = physical[c]
                    flow[index, 3 + c] = stream[c]
                    flow[index, 6 + c] = slope[c]
                    flow[index, 9 + c] = span[c]
                u, v, w = physical
            else:
                u, v, w = (flow[index, c] for c in range(3))
            u = u + heights[first_pair + index]
            total = []
            for c in range(3):
                value = u * stream[c] + v * slope[c] + w * span[c]
                if group > 0:
                    value += (
                        physical[0] * flow[index, 3 + c]
                        + physical[1] * flow[index, 6 + c]
                        + physical[2] * flow[index, 9 + c]
                    )
                if c == 0:
                    value += physical[1]
                total.append(value)
            in_k = mul(stacked(jnp.concatenate(total, axis=0), 1), z_back[...])
            in_k = jnp.concatenate([field(in_k, c) for c in range(3)], axis=1)
            in_m = mul(x_back[...], stacked(in_k, 0))
            for c in range(3):
                outgoing[group, index, c] = in_m[:, c * TILE : (c + 1) * TILE]
            spot = tile_at(first_pair + index)
            for hop in range(1, 8):
                other = lax.rem(place + hop, 8)
                pltpu.make_async_remote_copy(
                    src_ref=outgoing.at[
                        group, index, :, pl.ds(pl.multiple_of(other * 8, 8), 8), :
                    ],
                    dst_ref=returned.at[group, :, :, spot],
                    send_sem=back_send.at[group],
                    recv_sem=back_recv.at[group],
                    device_id=(seg, other),
                    device_id_type=MESH,
                ).start()
            returned[group, :, :, spot] = outgoing[
                group, index, :, pl.ds(pl.multiple_of(place * 8, 8), 8), :
            ]
            return carry

        wait_heights(0, group)
        wait_heights(1, group)
        lax.fori_loop(0, count, step, 0)

    def finish(group):
        wait_pairs(back_recv.at[group])
        rows = pl.ds(3 * group, 3)
        for pair in range(PAIRS):
            lanes = pl.ds(pair * TILE, TILE)
            value = keep * (fields[rows, :, lanes] + returned[group, :, :, lanes])
            forced[rows, :, lanes] = value
            turned[rows, :, lanes] = pltpu.roll(value, NZ, 2)
        across_heights(
            group, forced, turned, lambda pair, row: solve[pair, row], ends
        )

    transform(0)
    transform(1)
    finish(0)
    transform(2)
    finish(1)
    for copy in shift:
        copy.wait_recv()
    finish(2)

    def products(index, sums):
        lanes = tile_at(index)
        start = [fields[pl.ds(3 * g, 3), :, lanes] for g in range(3)]
        end = [ends[pl.ds(3 * g, 3), :, lanes] for g in range(3)]
        gap = [end[g] - later[pl.ds(3 * g, 3), :, lanes] for g in range(3)]
        for g in range(3):
            ends[pl.ds(3 * g, 3), :, lanes] = gap[g]
        drift = end[0] - start[0]
        terms = [
            drift * start[1],
            drift * start[2],
            gap[1] * gap[1],
            gap[2] * gap[2],
            gap[1] * gap[0],
            gap[2] * gap[0],
            gap[1] * gap[2],
        ]
        return tuple(s + t[0] + t[1] + t[2] for s, t in zip(sums, terms))

    sums = lax.fori_loop(
        0, PAIRS, products, tuple(jnp.zeros((8, TILE), jnp.float32) for _ in range(7))
    )
    row = lax.broadcasted_iota(jnp.int32, (1, TILE), 1)
    message = jnp.zeros((1, TILE), jnp.float32)
    for index, value in enumerate(sums):
        total = jnp.sum(jnp.sum(value, axis=0, keepdims=True), axis=1, keepdims=True)
        message = jnp.where(row == index, total, message)

    def exchange(which, slots, me, size, device, value):
        slots[me] = value
        for step in range(1, size):
            pltpu.make_async_remote_copy(
                src_ref=slots.at[me],
                dst_ref=slots.at[me],
                send_sem=sum_send.at[which],
                recv_sem=sum_recv.at[which],
                device_id=device(step),
                device_id_type=MESH,
            ).start()
        if size > 1:
            drain(slots.at[pl.ds(0, size - 1)], sum_recv.at[which])
        return jnp.sum(slots[...], axis=0)

    message = exchange(0, near, near_me, near_count, near_device, message)
    message = exchange(1, far, chip_pair, far_count, far_device, message)

    def number(index):
        return message[:, index : index + 1]

    root = 1.0 / math.sqrt(nseg * 3 * NX * LANES)
    border = [number(0) * root, number(1) * root]
    diag = [number(2) + border[0] * border[0], number(3) + border[1] * border[1]]
    first = [-number(4) / diag[0], -number(5) / diag[1]]
    cross = number(6) + border[0] * border[1]
    weight = [
        first[0] - first[1] * cross / diag[0],
        first[1] - first[0] * cross / diag[1],
    ]
    weight = [jnp.broadcast_to(value, (8, TILE)) for value in weight]

    def write(index, carry):
        lanes = tile_at(index)
        for source, target in ((fields, corrected), (ends, new_residual)):
            target[0, :, :, lanes] = (
                source[pl.ds(0, 3), :, lanes]
                + weight[0] * source[pl.ds(3, 3), :, lanes]
                + weight[1] * source[pl.ds(6, 3), :, lanes]
            )
        return carry

    lax.fori_loop(0, PAIRS, write, 0)

    for unit in range(2):
        for group in range(3):
            wait_pairs(out_send.at[unit, group])
    for group in range(3):
        @pl.when(count == 3)
        def _():
            drain(outgoing.at[group, pl.ds(0, 3), :, pl.ds(0, 56), :], back_send.at[group])

        @pl.when(count == 2)
        def _():
            drain(outgoing.at[group, pl.ds(0, 2), :, pl.ds(0, 56), :], back_send.at[group])

    for copy in shift:
        copy.wait_send()
    drain(near.at[pl.ds(0, near_count - 1)], sum_send.at[0])
    if far_count > 1:
        drain(far.at[pl.ds(0, far_count - 1)], sum_send.at[1])


def local(nseg, constants, states, tangent_panel, wall_inverse, keep_mask):
    operands = (
        states,
        tangent_panel,
        wall_inverse.reshape(8 * NY, NY),
        keep_mask,
        *[jnp.asarray(value) for value in constants],
    )
    f32 = jnp.float32
    sem = pltpu.SemaphoreType.DMA
    whole = (9, 8, LANES)
    scratch = [
        *[pltpu.VMEM(value.shape, value.dtype) for value in constants],
        pltpu.VMEM((8 * NY, NY), f32),
        pltpu.VMEM((NX, NZ), jnp.int32),
        pltpu.VMEM(whole, f32),
        pltpu.VMEM(whole, f32),
        pltpu.VMEM(whole, f32),
        pltpu.VMEM((2, 3, 3, 8, 8, 3 * TILE), f32),
        pltpu.VMEM((3, 12, NX, TILE), f32),
        pltpu.VMEM((3, 3, 3, NX, TILE), f32),
        pltpu.VMEM((3, 3, 8, LANES), f32),
        pltpu.VMEM((PAIRS, 2 * PAIRS, 8, TILE), f32),
        pltpu.VMEM(whole, f32),
        pltpu.VMEM(whole, f32),
        pltpu.VMEM(whole, f32),
        pltpu.VMEM(whole, f32),
        pltpu.VMEM((16, 1, TILE), f32),
        pltpu.VMEM((nseg // 2, 1, TILE), f32),
        sem((12,)),
        sem((2, 3)),
        sem((2, 3)),
        sem((3,)),
        sem((3,)),
        sem((3,)),
        sem((3,)),
        sem((2,)),
        sem((2,)),
    ]
    return pl.pallas_call(
        functools.partial(kernel, nseg),
        out_shape=[jax.ShapeDtypeStruct((1, 3, 8, LANES), f32)] * 2,
        in_specs=[pl.BlockSpec(memory_space=pl.ANY)] * len(operands),
        out_specs=[pl.BlockSpec(memory_space=pltpu.VMEM)] * 2,
        scratch_shapes=scratch,
        compiler_params=pltpu.CompilerParams(
            collective_id=0, has_side_effects=True, vmem_limit_bytes=48 * 1024 * 1024
        ),
        name="newton_step",
    )(*operands)


def solution(mesh):
    return jax.shard_map(
        functools.partial(local, mesh.shape["seg"], tables()),
        mesh=mesh,
        in_specs=(
            P("seg", None, "space", None),
            P("seg", None, None, "space", None),
            P("space", None, None),
            P(),
        ),
        out_specs=(P("seg", None, "space", None), P("seg", None, "space", None)),
        check_vma=False,
    )
```

```python
import functools
import math

import jax
import jax.numpy as jnp
import ml_dtypes
import numpy as np
from jax import lax
from jax.experimental import pallas as pl
from jax.experimental.pallas import tpu as pltpu
from jax.sharding import PartitionSpec as P

TIME_STEP = 0.005
VISCOSITY = 0.0025
STREAM_WAVE = 1.0
SPAN_WAVE = 2.0
MESH = pl.DeviceIdType.MESH
NX, NY, NZ = 64, 40, 64
TILE = 128
PAIRS = NY // 2
LANES = NY * NZ


def fourier_basis(length, stretch):
    mode = np.arange(length)[:, None]
    point = np.arange(length)[None, :]
    wave = np.where(mode == length - 1, length // 2, (mode + 1) // 2)
    phase = 2.0 * math.pi / length * (wave * point % length)
    edge = (mode == 0) | (mode == length - 1)
    amplitude = np.where(edge, math.sqrt(1.0 / length), math.sqrt(2.0 / length))
    cosine = (mode % 2 == 1) | (mode == 0)
    basis = amplitude * np.where(cosine, np.cos(phase), np.sin(phase))
    slope = stretch * wave * amplitude * np.where(cosine, -np.sin(phase), np.cos(phase))
    return basis, np.where(edge, 0.0, slope)


def wall_tables(length):
    index = np.arange(1, length + 1)
    height = np.cos(math.pi / (length + 1) * index)
    row, col = height[:, None], height[None, :]
    parity = np.where((index[:, None] + index[None, :]) % 2 == 0, 1.0, -1.0)
    same = index[:, None] == index[None, :]
    spacing = np.where(same, 1.0, row - col)
    return height, np.where(same, -row / (2.0 * (1.0 - row * row)), parity / spacing)


def span_damping(length):
    index = np.arange(length)
    wave = np.where(index == length - 1, length // 2, (index + 1) // 2)
    return 1.0 / (1.0 + TIME_STEP * VISCOSITY * (SPAN_WAVE * wave) ** 2)


def parts(matrix):
    high = matrix.astype(np.float32).astype(ml_dtypes.bfloat16)
    low = (matrix - high.astype(np.float64)).astype(np.float32).astype(ml_dtypes.bfloat16)
    return high, low


def twice(matrix):
    zero = np.zeros_like(matrix)
    return np.block([[matrix, zero], [zero, matrix]])


def tables():
    qx, sx = fourier_basis(NX, STREAM_WAVE)
    qz, sz = fourier_basis(NZ, SPAN_WAVE)
    height, wall = wall_tables(NY)
    high, low = parts(np.concatenate([qx.T, sx.T], axis=0))
    x_forward = np.concatenate([high, high, low], axis=1)
    high, low = parts(qx)
    x_back = np.concatenate([high, high, low], axis=1)
    high, low = parts(np.concatenate([twice(qz), twice(sz)], axis=1))
    z_forward = np.concatenate([high, high, low], axis=0)
    high, low = parts(-TIME_STEP * twice(qz.T))
    z_back = np.concatenate([high, high, low], axis=0)
    derivative = np.zeros((PAIRS, 2 * PAIRS, TILE))
    for half in (0, 1):
        lanes = slice(half * NZ, (half + 1) * NZ)
        derivative[:, 0::2, lanes] = wall[half::2, half::2][:, :, None]
        derivative[:, 1::2, lanes] = wall[half::2, 1 - half :: 2][:, :, None]
    heights = np.repeat(height.reshape(PAIRS, 1, 2), NZ, axis=2)
    damping = np.tile(span_damping(NZ), 2)[None, :]
    single = [value.astype(np.float32) for value in (derivative, heights, damping)]
    return (x_forward, x_back, z_forward, z_back, *single)


def band(place):
    row, side = lax.rem(place, 4), lax.div(place, 4)
    odd = lax.rem(row, 2)
    count = 3 - lax.rem(row + side, 2)
    return 5 * row + side * (3 - odd), count


def tile_at(index, tiles=1):
    return pl.ds(pl.multiple_of(index * TILE, TILE), tiles * TILE)


def split(value):
    high = value.astype(jnp.bfloat16)
    low = (value - high.astype(jnp.float32)).astype(jnp.bfloat16)
    return high, low


def stacked(value, axis):
    high, low = split(value)
    return jnp.concatenate([high, low, high], axis=axis)


def mul(a, b):
    return jnp.dot(a, b, preferred_element_type=jnp.float32)


def kernel(
    nseg,
    states,
    panel,
    wall,
    mask,
    x_forward_in,
    x_back_in,
    z_forward_in,
    z_back_in,
    derivative_in,
    heights_in,
    damping_in,
    corrected,
    new_residual,
    x_forward,
    x_back,
    z_forward,
    z_back,
    derivative,
    heights,
    damping,
    wall_v,
    mask_v,
    fields,
    swapped,
    slopes,
    got,
    flow,
    outgoing,
    returned,
    solve,
    forced,
    turned,
    ends,
    later,
    near,
    far,
    in_sem,
    out_send,
    out_recv,
    back_send,
    back_recv,
    later_send,
    later_recv,
    sum_send,
    sum_recv,
):
    seg = lax.axis_index("seg")
    place = lax.axis_index("space")
    core = lax.rem(seg, 2)
    chip_pair = lax.div(seg, 2)
    before = lax.rem(seg + nseg - 1, nseg)
    across = lax.rem(seg + nseg + 2 * core - 1, nseg)
    near_count, far_count = 16, nseg // 2
    near_me = core * 8 + place
    first_pair, count = band(place)

    def near_device(step):
        other = lax.rem(near_me + step, near_count)
        return (seg - core + lax.div(other, 8), lax.rem(other, 8))

    def far_device(step):
        return (2 * lax.rem(chip_pair + step, far_count) + core, place)

    barrier = pltpu.get_barrier_semaphore()
    for step in range(1, near_count):
        pl.semaphore_signal(barrier, inc=1, device_id=near_device(step), device_id_type=MESH)
    pl.semaphore_signal(barrier, inc=1, device_id=(across, place), device_id_type=MESH)
    for step in range(1, far_count):
        pl.semaphore_signal(barrier, inc=1, device_id=far_device(step), device_id_type=MESH)

    loads = [
        (states.at[0], fields.at[pl.ds(0, 3)]),
        (panel.at[0, 0], fields.at[pl.ds(3, 3)]),
        (panel.at[0, 1], fields.at[pl.ds(6, 3)]),
        (derivative_in, derivative),
        (wall, wall_v),
        (mask, mask_v),
        (x_forward_in, x_forward),
        (z_forward_in, z_forward),
        (x_back_in, x_back),
        (z_back_in, z_back),
        (heights_in, heights),
        (damping_in, damping),
    ]
    loads = [
        pltpu.make_async_copy(src, dst, in_sem.at[index])
        for index, (src, dst) in enumerate(loads)
    ]
    for load in loads:
        load.start()
    pl.semaphore_wait(barrier, near_count + far_count - 1)

    def send_heights(unit, group, source):
        for step in range(1, 8):
            other = lax.rem(place + step, 8)
            other_first, other_count = band(other)
            pltpu.make_async_remote_copy(
                src_ref=source.at[:, :, tile_at(other_first, 2)],
                dst_ref=got.at[unit, group, :, place, :, pl.ds(0, 2 * TILE)],
                send_sem=out_send.at[unit, group],
                recv_sem=out_recv.at[unit, group],
                device_id=(seg, other),
                device_id_type=MESH,
            ).start()

            @pl.when(other_count == 3)
            def _():
                pltpu.make_async_remote_copy(
                    src_ref=source.at[:, :, tile_at(other_first + 2)],
                    dst_ref=got.at[unit, group, :, place, :, pl.ds(2 * TILE, TILE)],
                    send_sem=out_send.at[unit, group],
                    recv_sem=out_recv.at[unit, group],
                    device_id=(seg, other),
                    device_id_type=MESH,
                ).start()

    def keep_heights(unit, group, source):
        got[unit, group, :, place, :, pl.ds(0, 2 * TILE)] = source[
            pl.ds(3 * group, 3), :, tile_at(first_pair, 2)
        ]

        @pl.when(count == 3)
        def _():
            got[unit, group, :, place, :, pl.ds(2 * TILE, TILE)] = source[
                pl.ds(3 * group, 3), :, tile_at(first_pair + 2)
            ]

    def drain(ref, sem):
        pltpu.make_async_copy(ref, ref, sem).wait()

    def wait_heights(unit, group):
        @pl.when(count == 3)
        def _():
            drain(
                got.at[unit, group, :, pl.ds(0, 7), :, pl.ds(0, 3 * TILE)],
                out_recv.at[unit, group],
            )

        @pl.when(count == 2)
        def _():
            drain(
                got.at[unit, group, :, pl.ds(0, 7), :, pl.ds(0, 2 * TILE)],
                out_recv.at[unit, group],
            )

    def wait_pairs(sem):
        @pl.when(count == 3)
        def _():
            drain(returned.at[0, :, :, pl.ds(0, (PAIRS - 3) * TILE)], sem)

        @pl.when(count == 2)
        def _():
            drain(returned.at[0, :, :, pl.ds(0, (PAIRS - 2) * TILE)], sem)

    def across_heights(group, source, other, coefficient, target):
        rows = pl.ds(3 * group, 3)

        def step(index, carry):
            sums = [jnp.zeros((3, 8, TILE), jnp.float32) for _ in range(2)]
            for pair in range(PAIRS):
                lanes = pl.ds(pair * TILE, TILE)
                straight, turned_pair = source[rows, :, lanes], other[rows, :, lanes]
                for which in range(2):
                    sums[which] += coefficient(2 * index + which, 2 * pair) * straight
                    sums[which] += coefficient(2 * index + which, 2 * pair + 1) * turned_pair
            target[rows, :, tile_at(2 * index)] = sums[0]
            target[rows, :, tile_at(2 * index + 1)] = sums[1]
            return carry

        lax.fori_loop(0, PAIRS // 2, step, 0)

    def turn(group, source, target):
        rows = pl.ds(3 * group, 3)
        for pair in range(PAIRS):
            lanes = pl.ds(pair * TILE, TILE)
            target[rows, :, lanes] = pltpu.roll(source[rows, :, lanes], NZ, 2)

    for group in range(3):
        source = states.at[0] if group == 0 else panel.at[0, group - 1]
        send_heights(0, group, source)
        loads[group].wait()
        if group == 0:
            loads[3].wait()
        turn(group, fields, swapped)
        across_heights(
            group,
            fields,
            swapped,
            lambda pair, row: derivative[pair, pl.ds(row, 1), :],
            slopes,
        )
        send_heights(1, group, slopes.at[pl.ds(3 * group, 3)])
        keep_heights(0, group, fields)
        keep_heights(1, group, slopes)

    shift = [
        pltpu.make_async_remote_copy(
            src_ref=src,
            dst_ref=dst,
            send_sem=later_send.at[index],
            recv_sem=later_recv.at[index],
            device_id=(before, place),
            device_id_type=MESH,
        )
        for index, (src, dst) in enumerate(
            [
                (states.at[0], later.at[pl.ds(0, 3)]),
                (panel.at[0, 0], later.at[pl.ds(3, 3)]),
                (panel.at[0, 1], later.at[pl.ds(6, 3)]),
            ]
        )
    ]
    for copy in shift:
        copy.start()
    for load in loads[4:]:
        load.wait()

    lane = lax.broadcasted_iota(jnp.int32, (8, TILE), 1)
    low_half = lane < NZ

    def solve_rows(pair, carry):
        even = wall_v[pl.ds(2 * pair, 8, stride=NY), :]
        odd = wall_v[pl.ds(2 * pair + 1, 8, stride=NY), :]

        def spread(value, column):
            return jnp.broadcast_to(value[:, column : column + 1], (8, TILE))

        for other in range(PAIRS):
            solve[pair, 2 * other] = jnp.where(
                low_half, spread(even, 2 * other), spread(odd, 2 * other + 1)
            )
            solve[pair, 2 * other + 1] = jnp.where(
                low_half, spread(even, 2 * other + 1), spread(odd, 2 * other)
            )
        return carry

    lax.fori_loop(0, PAIRS, solve_rows, 0)

    own_rows = mask_v[pl.ds(pl.multiple_of(place * 8, 8), 8), :].astype(jnp.float32)
    keep = jnp.concatenate([own_rows, own_rows], axis=1) * damping[...]

    def transform(group):
        wait_heights(0, group)
        wait_heights(1, group)

        def modes(unit):
            value = got[unit, group].reshape(3, NX, 3 * TILE)
            return stacked(jnp.concatenate([value[0], value[1], value[2]], axis=1), 0)

        def by_rows(value):
            return [value[:, c * TILE : (c + 1) * TILE] for c in range(9)]

        in_x = mul(x_forward[...], modes(0))
        in_x_wall = mul(x_forward[pl.ds(0, NX), :], modes(1))
        plain = jnp.concatenate(by_rows(in_x[:NX]), axis=0)
        rest = jnp.concatenate(by_rows(in_x[NX:]) + by_rows(in_x_wall), axis=0)
        pair = mul(stacked(plain, 1), z_forward[...])
        single = mul(stacked(rest, 1), z_forward[:, pl.ds(0, TILE)])
        total = [None] * 9
        for index in range(3):

            def field(value, c):
                row = (3 * c + index) * NX
                return value[row : row + NX]

            physical = [field(pair[:, :TILE], c) for c in range(3)]
            span = [field(pair[:, TILE:], c) for c in range(3)]
            stream = [field(single, c) for c in range(3)]
            slope = [field(single, c + 3) for c in range(3)]
            if group == 0:
                for c in range(3):
                    flow[index, c] = physical[c]
                    flow[index, 3 + c] = stream[c]
                    flow[index, 6 + c] = slope[c]
                    flow[index, 9 + c] = span[c]
                u, v, w = physical
            else:
                u, v, w = (flow[index, c] for c in range(3))
            u = u + heights[lax.min(first_pair + index, PAIRS - 1)]
            for c in range(3):
                value = u * stream[c] + v * slope[c] + w * span[c]
                if group > 0:
                    value += (
                        physical[0] * flow[index, 3 + c]
                        + physical[1] * flow[index, 6 + c]
                        + physical[2] * flow[index, 9 + c]
                    )
                if c == 0:
                    value += physical[1]
                total[3 * c + index] = value
        in_k = mul(stacked(jnp.concatenate(total, axis=0), 1), z_back[...])
        in_k = jnp.concatenate([in_k[c * NX : (c + 1) * NX] for c in range(9)], axis=1)
        in_m = mul(x_back[...], stacked(in_k, 0))
        for c in range(3):
            outgoing[group, c] = in_m[:, 3 * c * TILE : 3 * (c + 1) * TILE]
        for hop in range(1, 8):
            other = lax.rem(place + hop, 8)
            rows = pl.ds(pl.multiple_of(other * 8, 8), 8)

            def send(start, tiles):
                pltpu.make_async_remote_copy(
                    src_ref=outgoing.at[group, :, rows, pl.ds(start * TILE, tiles * TILE)],
                    dst_ref=returned.at[group, :, :, tile_at(first_pair + start, tiles)],
                    send_sem=back_send.at[group],
                    recv_sem=back_recv.at[group],
                    device_id=(seg, other),
                    device_id_type=MESH,
                ).start()

            send(0, 2)

            @pl.when(count == 3)
            def _():
                send(2, 1)

        own = pl.ds(pl.multiple_of(place * 8, 8), 8)
        returned[group, :, :, tile_at(first_pair, 2)] = outgoing[
            group, :, own, pl.ds(0, 2 * TILE)
        ]

        @pl.when(count == 3)
        def _():
            returned[group, :, :, tile_at(first_pair + 2)] = outgoing[
                group, :, own, pl.ds(2 * TILE, TILE)
            ]

    def finish(group):
        wait_pairs(back_recv.at[group])
        rows = pl.ds(3 * group, 3)
        for pair in range(PAIRS):
            lanes = pl.ds(pair * TILE, TILE)
            value = keep * (fields[rows, :, lanes] + returned[group, :, :, lanes])
            forced[rows, :, lanes] = value
            turned[rows, :, lanes] = pltpu.roll(value, NZ, 2)
        across_heights(
            group, forced, turned, lambda pair, row: solve[pair, row], ends
        )

    transform(0)
    transform(1)
    finish(0)
    transform(2)
    finish(1)
    for copy in shift:
        copy.wait_recv()
    finish(2)

    def products(index, sums):
        lanes = tile_at(index)
        start = [fields[pl.ds(3 * g, 3), :, lanes] for g in range(3)]
        end = [ends[pl.ds(3 * g, 3), :, lanes] for g in range(3)]
        gap = [end[g] - later[pl.ds(3 * g, 3), :, lanes] for g in range(3)]
        for g in range(3):
            ends[pl.ds(3 * g, 3), :, lanes] = gap[g]
        drift = end[0] - start[0]
        terms = [
            drift * start[1],
            drift * start[2],
            gap[1] * gap[1],
            gap[2] * gap[2],
            gap[1] * gap[0],
            gap[2] * gap[0],
            gap[1] * gap[2],
        ]
        return tuple(s + t[0] + t[1] + t[2] for s, t in zip(sums, terms))

    sums = lax.fori_loop(
        0, PAIRS, products, tuple(jnp.zeros((8, TILE), jnp.float32) for _ in range(7))
    )
    row = lax.broadcasted_iota(jnp.int32, (1, TILE), 1)
    message = jnp.zeros((1, TILE), jnp.float32)
    for index, value in enumerate(sums):
        total = jnp.sum(jnp.sum(value, axis=0, keepdims=True), axis=1, keepdims=True)
        message = jnp.where(row == index, total, message)

    def exchange(which, slots, me, size, device, value):
        slots[me] = value
        for step in range(1, size):
            pltpu.make_async_remote_copy(
                src_ref=slots.at[me],
                dst_ref=slots.at[me],
                send_sem=sum_send.at[which],
                recv_sem=sum_recv.at[which],
                device_id=device(step),
                device_id_type=MESH,
            ).start()
        if size > 1:
            drain(slots.at[pl.ds(0, size - 1)], sum_recv.at[which])
        return jnp.sum(slots[...], axis=0)

    message = exchange(0, near, near_me, near_count, near_device, message)
    message = exchange(1, far, chip_pair, far_count, far_device, message)

    def number(index):
        return message[:, index : index + 1]

    root = 1.0 / math.sqrt(nseg * 3 * NX * LANES)
    border = [number(0) * root, number(1) * root]
    diag = [number(2) + border[0] * border[0], number(3) + border[1] * border[1]]
    first = [-number(4) / diag[0], -number(5) / diag[1]]
    cross = number(6) + border[0] * border[1]
    weight = [
        first[0] - first[1] * cross / diag[0],
        first[1] - first[0] * cross / diag[1],
    ]
    weight = [jnp.broadcast_to(value, (8, TILE)) for value in weight]

    def write(index, carry):
        lanes = tile_at(index)
        for source, target in ((fields, corrected), (ends, new_residual)):
            target[0, :, :, lanes] = (
                source[pl.ds(0, 3), :, lanes]
                + weight[0] * source[pl.ds(3, 3), :, lanes]
                + weight[1] * source[pl.ds(6, 3), :, lanes]
            )
        return carry

    lax.fori_loop(0, PAIRS, write, 0)

    for unit in range(2):
        for group in range(3):
            wait_pairs(out_send.at[unit, group])
    for group in range(3):
        @pl.when(count == 3)
        def _():
            drain(outgoing.at[group, :, pl.ds(0, 56), pl.ds(0, 3 * TILE)], back_send.at[group])

        @pl.when(count == 2)
        def _():
            drain(outgoing.at[group, :, pl.ds(0, 56), pl.ds(0, 2 * TILE)], back_send.at[group])

    for copy in shift:
        copy.wait_send()
    drain(near.at[pl.ds(0, near_count - 1)], sum_send.at[0])
    if far_count > 1:
        drain(far.at[pl.ds(0, far_count - 1)], sum_send.at[1])


def local(nseg, constants, states, tangent_panel, wall_inverse, keep_mask):
    operands = (
        states,
        tangent_panel,
        wall_inverse.reshape(8 * NY, NY),
        keep_mask,
        *[jnp.asarray(value) for value in constants],
    )
    f32 = jnp.float32
    sem = pltpu.SemaphoreType.DMA
    whole = (9, 8, LANES)
    scratch = [
        *[pltpu.VMEM(value.shape, value.dtype) for value in constants],
        pltpu.VMEM((8 * NY, NY), f32),
        pltpu.VMEM((NX, NZ), jnp.int32),
        pltpu.VMEM(whole, f32),
        pltpu.VMEM(whole, f32),
        pltpu.VMEM(whole, f32),
        pltpu.VMEM((2, 3, 3, 8, 8, 3 * TILE), f32),
        pltpu.VMEM((3, 12, NX, TILE), f32),
        pltpu.VMEM((3, 3, NX, 3 * TILE), f32),
        pltpu.VMEM((3, 3, 8, LANES), f32),
        pltpu.VMEM((PAIRS, 2 * PAIRS, 8, TILE), f32),
        pltpu.VMEM(whole, f32),
        pltpu.VMEM(whole, f32),
        pltpu.VMEM(whole, f32),
        pltpu.VMEM(whole, f32),
        pltpu.VMEM((16, 1, TILE), f32),
        pltpu.VMEM((nseg // 2, 1, TILE), f32),
        sem((12,)),
        sem((2, 3)),
        sem((2, 3)),
        sem((3,)),
        sem((3,)),
        sem((3,)),
        sem((3,)),
        sem((2,)),
        sem((2,)),
    ]
    return pl.pallas_call(
        functools.partial(kernel, nseg),
        out_shape=[jax.ShapeDtypeStruct((1, 3, 8, LANES), f32)] * 2,
        in_specs=[pl.BlockSpec(memory_space=pl.ANY)] * len(operands),
        out_specs=[pl.BlockSpec(memory_space=pltpu.VMEM)] * 2,
        scratch_shapes=scratch,
        compiler_params=pltpu.CompilerParams(
            collective_id=0, has_side_effects=True, vmem_limit_bytes=64 * 1024 * 1024
        ),
        name="newton_step",
    )(*operands)


def solution(mesh):
    return jax.shard_map(
        functools.partial(local, mesh.shape["seg"], tables()),
        mesh=mesh,
        in_specs=(
            P("seg", None, "space", None),
            P("seg", None, None, "space", None),
            P("space", None, None),
            P(),
        ),
        out_specs=(P("seg", None, "space", None), P("seg", None, "space", None)),
        check_vma=False,
    )
```

```python
import functools
import math

import jax
import jax.numpy as jnp
import ml_dtypes
import numpy as np
from jax import lax
from jax.experimental import pallas as pl
from jax.experimental.pallas import tpu as pltpu
from jax.sharding import PartitionSpec as P

TIME_STEP = 0.005
VISCOSITY = 0.0025
STREAM_WAVE = 1.0
SPAN_WAVE = 2.0
MESH = pl.DeviceIdType.MESH
NX, NY, NZ = 64, 40, 64
TILE = 128
PAIRS = NY // 2
LANES = NY * NZ


def fourier_basis(length, stretch):
    mode = np.arange(length)[:, None]
    point = np.arange(length)[None, :]
    wave = np.where(mode == length - 1, length // 2, (mode + 1) // 2)
    phase = 2.0 * math.pi / length * (wave * point % length)
    edge = (mode == 0) | (mode == length - 1)
    amplitude = np.where(edge, math.sqrt(1.0 / length), math.sqrt(2.0 / length))
    cosine = (mode % 2 == 1) | (mode == 0)
    basis = amplitude * np.where(cosine, np.cos(phase), np.sin(phase))
    slope = stretch * wave * amplitude * np.where(cosine, -np.sin(phase), np.cos(phase))
    return basis, np.where(edge, 0.0, slope)


def wall_tables(length):
    index = np.arange(1, length + 1)
    height = np.cos(math.pi / (length + 1) * index)
    row, col = height[:, None], height[None, :]
    parity = np.where((index[:, None] + index[None, :]) % 2 == 0, 1.0, -1.0)
    same = index[:, None] == index[None, :]
    spacing = np.where(same, 1.0, row - col)
    return height, np.where(same, -row / (2.0 * (1.0 - row * row)), parity / spacing)


def span_damping(length):
    index = np.arange(length)
    wave = np.where(index == length - 1, length // 2, (index + 1) // 2)
    return 1.0 / (1.0 + TIME_STEP * VISCOSITY * (SPAN_WAVE * wave) ** 2)


def parts(matrix):
    high = matrix.astype(np.float32).astype(ml_dtypes.bfloat16)
    low = (matrix - high.astype(np.float64)).astype(np.float32).astype(ml_dtypes.bfloat16)
    return high, low


def twice(matrix):
    zero = np.zeros_like(matrix)
    return np.block([[matrix, zero], [zero, matrix]])


def tables():
    qx, sx = fourier_basis(NX, STREAM_WAVE)
    qz, sz = fourier_basis(NZ, SPAN_WAVE)
    height, wall = wall_tables(NY)
    high, low = parts(np.concatenate([qx.T, sx.T], axis=0))
    x_forward = np.concatenate([high, high, low], axis=1)
    high, low = parts(qx)
    x_back = np.concatenate([high, high, low], axis=1)
    high, low = parts(np.concatenate([twice(qz), twice(sz)], axis=1))
    z_forward = np.concatenate([high, high, low], axis=0)
    high, low = parts(-TIME_STEP * twice(qz.T))
    z_back = np.concatenate([high, high, low], axis=0)
    derivative = np.zeros((PAIRS, 2 * PAIRS, TILE))
    for half in (0, 1):
        lanes = slice(half * NZ, (half + 1) * NZ)
        derivative[:, 0::2, lanes] = wall[half::2, half::2][:, :, None]
        derivative[:, 1::2, lanes] = wall[half::2, 1 - half :: 2][:, :, None]
    heights = np.repeat(height.reshape(PAIRS, 1, 2), NZ, axis=2)
    damping = np.tile(span_damping(NZ), 2)[None, :]
    single = [value.astype(np.float32) for value in (derivative, heights, damping)]
    return (x_forward, x_back, z_forward, z_back, *single)


def band(place):
    row, side = lax.rem(place, 4), lax.div(place, 4)
    odd = lax.rem(row, 2)
    count = 3 - lax.rem(row + side, 2)
    return 5 * row + side * (3 - odd), count


def tile_at(index, tiles=1):
    return pl.ds(pl.multiple_of(index * TILE, TILE), tiles * TILE)


def split(value):
    high = value.astype(jnp.bfloat16)
    low = (value - high.astype(jnp.float32)).astype(jnp.bfloat16)
    return high, low


def stacked(value, axis):
    high, low = split(value)
    return jnp.concatenate([high, low, high], axis=axis)


def mul(a, b):
    return jnp.dot(a, b, preferred_element_type=jnp.float32)


def kernel(
    nseg,
    states,
    panel,
    wall,
    mask,
    x_forward_in,
    x_back_in,
    z_forward_in,
    z_back_in,
    derivative_in,
    heights_in,
    damping_in,
    corrected,
    new_residual,
    x_forward,
    x_back,
    z_forward,
    z_back,
    derivative,
    heights,
    damping,
    wall_v,
    mask_v,
    home,
    fields,
    swapped,
    slopes,
    got,
    passing,
    flow,
    outgoing,
    passing_back,
    returned,
    solve,
    forced,
    turned,
    ends,
    later,
    gaps,
    gaps_home,
    near,
    far,
    in_sem,
    trade_send,
    trade_recv,
    out_send,
    out_recv,
    pass_send,
    pass_recv,
    back_send,
    back_recv,
    pass_back_send,
    pass_back_recv,
    later_send,
    later_recv,
    home_send,
    home_recv,
    sum_send,
    sum_recv,
):
    seg = lax.axis_index("seg")
    space = lax.axis_index("space")
    core = lax.rem(seg, 2)
    side = lax.div(space, 4)
    row = lax.rem(space, 4)
    base = seg - core
    chip_pair = lax.div(seg, 2)
    near_count, far_count = 16, nseg // 2
    near_me = core * 8 + space
    place = core * 4 + row
    traded = core + side == 1
    trader = (base + side, place)
    first_pair, count = band(place)

    def near_device(step):
        other = lax.rem(near_me + step, near_count)
        return (base + lax.div(other, 8), lax.rem(other, 8))

    def far_device(step):
        return (2 * lax.rem(chip_pair + step, far_count) + core, space)

    def member(kind, hop):
        where = lax.rem(row + hop + 4, 4)
        return kind * 4 + where, (base + kind, side * 4 + where)

    next_pair = lax.rem(seg + 2 * side - 2 * (1 - side) + nseg, nseg)
    across = (next_pair, space + 4 * (1 - side) - 4 * side)

    barrier = pltpu.get_barrier_semaphore()
    for step in range(1, near_count):
        pl.semaphore_signal(barrier, inc=1, device_id=near_device(step), device_id_type=MESH)
    pl.semaphore_signal(barrier, inc=1, device_id=across, device_id_type=MESH)
    for step in range(1, far_count):
        pl.semaphore_signal(barrier, inc=1, device_id=far_device(step), device_id_type=MESH)

    own = [states.at[0], panel.at[0, 0], panel.at[0, 1]]

    def group_rows(group):
        return pl.ds(3 * group, 3)

    loads = [
        (derivative_in, derivative),
        (mask, mask_v),
        (x_forward_in, x_forward),
        (z_forward_in, z_forward),
        (x_back_in, x_back),
        (z_back_in, z_back),
        (heights_in, heights),
        (damping_in, damping),
        *[(own[group], home.at[group_rows(group)]) for group in range(3)],
    ]
    loads = [
        pltpu.make_async_copy(src, dst, in_sem.at[index])
        for index, (src, dst) in enumerate(loads)
    ]
    begins = [(own[group], fields.at[group_rows(group)]) for group in range(3)] + [(wall, wall_v)]

    @pl.when(jnp.logical_not(traded))
    def _():
        for index, (src, dst) in enumerate(begins):
            pltpu.make_async_copy(src, dst, trade_recv.at[index]).start()

    for load in loads:
        load.start()
    pl.semaphore_wait(barrier, near_count + far_count - 1)

    def send(src, dst, send_sem, recv_sem, device):
        pltpu.make_async_remote_copy(
            src_ref=src,
            dst_ref=dst,
            send_sem=send_sem,
            recv_sem=recv_sem,
            device_id=device,
            device_id_type=MESH,
        ).start()

    def send_tiles(src, dst, three, send_sem, recv_sem, device):
        send(src(0, 2), dst(0, 2), send_sem, recv_sem, device)

        @pl.when(three)
        def _():
            send(src(2, 1), dst(2, 1), send_sem, recv_sem, device)

    @pl.when(traded)
    def _():
        for index, (src, dst) in enumerate(begins):
            send(src, dst, trade_send.at[index], trade_recv.at[index], trader)

    def slot(ref, *index):
        return lambda start, tiles: ref.at[(*index, pl.ds(start * TILE, tiles * TILE))]

    def band_of(ref, first, *index):
        return lambda start, tiles: ref.at[(*index, tile_at(first + start, tiles))]

    everything = slice(None)
    direct = [(1 - core, 0), (0, 1), (1, 1), (0, 3), (1, 3)]
    opposite = [(0, 1), (1, 3)]

    def send_heights(unit, group, source):
        sems = out_send.at[unit, group]
        for way, (kind, hop) in enumerate(opposite):
            other, _ = member(kind, 2)
            _, relay = member(core, hop)
            other_first, other_count = band(other)
            send_tiles(
                band_of(source, other_first, everything, everything),
                slot(passing, unit, group, way, everything, everything),
                other_count == 3,
                sems,
                pass_recv.at[unit, group, way],
                relay,
            )
        for kind, hop in direct:
            other, device = member(kind, hop)
            other_first, other_count = band(other)
            send_tiles(
                band_of(source, other_first, everything, everything),
                slot(got, unit, group, everything, place, everything),
                other_count == 3,
                sems,
                out_recv.at[unit, group],
                device,
            )

    def drain_tiles(ref, three, sem):
        @pl.when(three)
        def _():
            drain(ref(0, 3), sem)

        @pl.when(jnp.logical_not(three))
        def _():
            drain(ref(0, 2), sem)

    def pass_heights(unit, group):
        for way, (kind, hop) in enumerate(opposite):
            origin, _ = member(core, hop + 2)
            other, device = member(kind, hop)
            _, other_count = band(other)
            held = slot(passing, unit, group, way, everything, everything)
            drain_tiles(held, other_count == 3, pass_recv.at[unit, group, way])
            send_tiles(
                held,
                slot(got, unit, group, everything, origin, everything),
                other_count == 3,
                pass_send.at[unit, group, way],
                out_recv.at[unit, group],
                device,
            )

    def keep_heights(unit, group, source):
        got[unit, group, :, place, :, pl.ds(0, 2 * TILE)] = source[
            group_rows(group), :, tile_at(first_pair, 2)
        ]

        @pl.when(count == 3)
        def _():
            got[unit, group, :, place, :, pl.ds(2 * TILE, TILE)] = source[
                group_rows(group), :, tile_at(first_pair + 2)
            ]

    def drain(ref, sem):
        pltpu.make_async_copy(ref, ref, sem).wait()

    def wait_heights(unit, group):
        @pl.when(count == 3)
        def _():
            drain(
                got.at[unit, group, :, pl.ds(0, 7), :, pl.ds(0, 3 * TILE)],
                out_recv.at[unit, group],
            )

        @pl.when(count == 2)
        def _():
            drain(
                got.at[unit, group, :, pl.ds(0, 7), :, pl.ds(0, 2 * TILE)],
                out_recv.at[unit, group],
            )

    def wait_pairs(sem):
        @pl.when(count == 3)
        def _():
            drain(returned.at[0, :, :, pl.ds(0, (PAIRS - 3) * TILE)], sem)

        @pl.when(count == 2)
        def _():
            drain(returned.at[0, :, :, pl.ds(0, (PAIRS - 2) * TILE)], sem)

    def across_heights(group, source, other, coefficient, target):
        rows = pl.ds(3 * group, 3)

        def step(index, carry):
            sums = [jnp.zeros((3, 8, TILE), jnp.float32) for _ in range(2)]
            for pair in range(PAIRS):
                lanes = pl.ds(pair * TILE, TILE)
                straight, turned_pair = source[rows, :, lanes], other[rows, :, lanes]
                for which in range(2):
                    sums[which] += coefficient(2 * index + which, 2 * pair) * straight
                    sums[which] += coefficient(2 * index + which, 2 * pair + 1) * turned_pair
            target[rows, :, tile_at(2 * index)] = sums[0]
            target[rows, :, tile_at(2 * index + 1)] = sums[1]
            return carry

        lax.fori_loop(0, PAIRS // 2, step, 0)

    def turn(group, source, target):
        rows = pl.ds(3 * group, 3)
        for pair in range(PAIRS):
            lanes = pl.ds(pair * TILE, TILE)
            target[rows, :, lanes] = pltpu.roll(source[rows, :, lanes], NZ, 2)

    def begin(group):
        drain(fields.at[group_rows(group)], trade_recv.at[group])
        send_heights(0, group, fields.at[group_rows(group)])
        keep_heights(0, group, fields)

    def differentiate(group):
        turn(group, fields, swapped)
        across_heights(
            group,
            fields,
            swapped,
            lambda pair, row: derivative[pair, pl.ds(row, 1), :],
            slopes,
        )

    def send_slopes(group):
        send_heights(1, group, slopes.at[group_rows(group)])
        keep_heights(1, group, slopes)

    def send_start(sources, device):
        for group in range(3):
            send(
                sources[group],
                later.at[group_rows(group)],
                later_send.at[group],
                later_recv.at[group],
                device,
            )

    def shift():
        mine = [fields.at[group_rows(group)] for group in range(3)]

        @pl.when(side == 0)
        def _():
            send_start(mine, across)

        @pl.when(core * side == 1)
        def _():
            send_start(mine, (seg, space - 4))

        @pl.when(core * (1 - side) == 1)
        def _():
            for group in range(3):
                send(
                    own[group],
                    later.at[group_rows(group)],
                    home_send.at[3 + group],
                    later_recv.at[group],
                    (seg - 1, space),
                )

    lane = lax.broadcasted_iota(jnp.int32, (8, TILE), 1)
    low_half = lane < NZ

    def solve_rows(pair, carry):
        even = wall_v[pl.ds(2 * pair, 8, stride=NY), :]
        odd = wall_v[pl.ds(2 * pair + 1, 8, stride=NY), :]

        def spread(value, column):
            return jnp.broadcast_to(value[:, column : column + 1], (8, TILE))

        for other in range(PAIRS):
            solve[pair, 2 * other] = jnp.where(
                low_half, spread(even, 2 * other), spread(odd, 2 * other + 1)
            )
            solve[pair, 2 * other + 1] = jnp.where(
                low_half, spread(even, 2 * other + 1), spread(odd, 2 * other)
            )
        return carry

    def kept():
        rows = mask_v[pl.ds(pl.multiple_of(place * 8, 8), 8), :].astype(jnp.float32)
        return jnp.concatenate([rows, rows], axis=1) * damping[...]

    def transform(group):
        wait_heights(0, group)
        wait_heights(1, group)

        def modes(unit):
            value = got[unit, group].reshape(3, NX, 3 * TILE)
            return stacked(jnp.concatenate([value[0], value[1], value[2]], axis=1), 0)

        def by_rows(value):
            return [value[:, c * TILE : (c + 1) * TILE] for c in range(9)]

        in_x = mul(x_forward[...], modes(0))
        in_x_wall = mul(x_forward[pl.ds(0, NX), :], modes(1))
        plain = jnp.concatenate(by_rows(in_x[:NX]), axis=0)
        rest = jnp.concatenate(by_rows(in_x[NX:]) + by_rows(in_x_wall), axis=0)
        pair = mul(stacked(plain, 1), z_forward[...])
        single = mul(stacked(rest, 1), z_forward[:, pl.ds(0, TILE)])
        total = [None] * 9
        for index in range(3):

            def field(value, c):
                row = (3 * c + index) * NX
                return value[row : row + NX]

            physical = [field(pair[:, :TILE], c) for c in range(3)]
            span = [field(pair[:, TILE:], c) for c in range(3)]
            stream = [field(single, c) for c in range(3)]
            slope = [field(single, c + 3) for c in range(3)]
            if group == 0:
                for c in range(3):
                    flow[index, c] = physical[c]
                    flow[index, 3 + c] = stream[c]
                    flow[index, 6 + c] = slope[c]
                    flow[index, 9 + c] = span[c]
                u, v, w = physical
            else:
                u, v, w = (flow[index, c] for c in range(3))
            u = u + heights[lax.min(first_pair + index, PAIRS - 1)]
            for c in range(3):
                value = u * stream[c] + v * slope[c] + w * span[c]
                if group > 0:
                    value += (
                        physical[0] * flow[index, 3 + c]
                        + physical[1] * flow[index, 6 + c]
                        + physical[2] * flow[index, 9 + c]
                    )
                if c == 0:
                    value += physical[1]
                total[3 * c + index] = value
        in_k = mul(stacked(jnp.concatenate(total, axis=0), 1), z_back[...])
        in_k = jnp.concatenate([in_k[c * NX : (c + 1) * NX] for c in range(9)], axis=1)
        in_m = mul(x_back[...], stacked(in_k, 0))
        for c in range(3):
            outgoing[group, c] = in_m[:, 3 * c * TILE : 3 * (c + 1) * TILE]

        def rows_of(other):
            return pl.ds(pl.multiple_of(other * 8, 8), 8)

        for way, (kind, hop) in enumerate(opposite):
            other, _ = member(kind, 2)
            _, relay = member(core, hop)
            send_tiles(
                slot(outgoing, group, everything, rows_of(other)),
                slot(passing_back, group, way, everything, everything),
                count == 3,
                back_send.at[group],
                pass_back_recv.at[group, way],
                relay,
            )
        for kind, hop in direct:
            other, device = member(kind, hop)
            send_tiles(
                slot(outgoing, group, everything, rows_of(other)),
                band_of(returned, first_pair, group, everything, everything),
                count == 3,
                back_send.at[group],
                back_recv.at[group],
                device,
            )

        mine = rows_of(place)
        returned[group, :, :, tile_at(first_pair, 2)] = outgoing[
            group, :, mine, pl.ds(0, 2 * TILE)
        ]

        @pl.when(count == 3)
        def _():
            returned[group, :, :, tile_at(first_pair + 2)] = outgoing[
                group, :, mine, pl.ds(2 * TILE, TILE)
            ]

    def pass_back(group):
        for way, (kind, hop) in enumerate(opposite):
            origin, _ = member(core, hop + 2)
            _, device = member(kind, hop)
            origin_first, origin_count = band(origin)
            held = slot(passing_back, group, way, everything, everything)
            drain_tiles(held, origin_count == 3, pass_back_recv.at[group, way])
            send_tiles(
                held,
                band_of(returned, origin_first, group, everything, everything),
                origin_count == 3,
                pass_back_send.at[group, way],
                back_recv.at[group],
                device,
            )

    def finish(group, keep):
        wait_pairs(back_recv.at[group])
        rows = group_rows(group)
        for pair in range(PAIRS):
            lanes = pl.ds(pair * TILE, TILE)
            value = keep * (fields[rows, :, lanes] + returned[group, :, :, lanes])
            forced[rows, :, lanes] = value
            turned[rows, :, lanes] = pltpu.roll(value, NZ, 2)
        across_heights(
            group, forced, turned, lambda pair, row: solve[pair, row], ends
        )
        drain(later.at[rows], later_recv.at[group])
        gap = ends[rows] - later[rows]
        gaps[rows] = gap

        @pl.when(traded)
        def _():
            send(
                gaps.at[rows],
                gaps_home.at[rows],
                home_send.at[group],
                home_recv.at[group],
                trader,
            )

        @pl.when(jnp.logical_not(traded))
        def _():
            gaps_home[rows] = gap

    begin(0)
    loads[0].wait()
    differentiate(0)
    send_slopes(0)
    pass_heights(0, 0)
    begin(1)
    differentiate(1)
    pass_heights(1, 0)
    send_slopes(1)
    drain(wall_v, trade_recv.at[3])
    lax.fori_loop(0, PAIRS, solve_rows, 0)
    pass_heights(0, 1)
    begin(2)
    differentiate(2)
    pass_heights(1, 1)
    send_slopes(2)
    shift()
    for load in loads[1:]:
        load.wait()
    keep = kept()
    pass_heights(0, 2)
    transform(0)
    pass_heights(1, 2)
    transform(1)
    pass_back(0)
    transform(2)
    pass_back(1)
    finish(0, keep)
    pass_back(2)
    finish(1, keep)
    finish(2, keep)

    def products(index, sums):
        lanes = tile_at(index)
        start = [fields[group_rows(g), :, lanes] for g in range(3)]
        gap = [gaps[group_rows(g), :, lanes] for g in range(3)]
        drift = ends[group_rows(0), :, lanes] - start[0]
        terms = [
            drift * start[1],
            drift * start[2],
            gap[1] * gap[1],
            gap[2] * gap[2],
            gap[1] * gap[0],
            gap[2] * gap[0],
            gap[1] * gap[2],
        ]
        return tuple(s + t[0] + t[1] + t[2] for s, t in zip(sums, terms))

    sums = lax.fori_loop(
        0, PAIRS, products, tuple(jnp.zeros((8, TILE), jnp.float32) for _ in range(7))
    )
    column = lax.broadcasted_iota(jnp.int32, (1, TILE), 1)
    message = jnp.zeros((1, TILE), jnp.float32)
    for index, value in enumerate(sums):
        total = jnp.sum(jnp.sum(value, axis=0, keepdims=True), axis=1, keepdims=True)
        message = jnp.where(column == index, total, message)

    def exchange(which, slots, me, size, device, value):
        slots[me] = value
        for step in range(1, size):
            pltpu.make_async_remote_copy(
                src_ref=slots.at[me],
                dst_ref=slots.at[me],
                send_sem=sum_send.at[which],
                recv_sem=sum_recv.at[which],
                device_id=device(step),
                device_id_type=MESH,
            ).start()
        if size > 1:
            drain(slots.at[pl.ds(0, size - 1)], sum_recv.at[which])
        return jnp.sum(slots[...], axis=0)

    message = exchange(0, near, near_me, near_count, near_device, message)
    message = exchange(1, far, chip_pair, far_count, far_device, message)

    def number(index):
        return message[:, index : index + 1]

    root = 1.0 / math.sqrt(nseg * 3 * NX * LANES)
    border = [number(0) * root, number(1) * root]
    diag = [number(2) + border[0] * border[0], number(3) + border[1] * border[1]]
    first = [-number(4) / diag[0], -number(5) / diag[1]]
    cross = number(6) + border[0] * border[1]
    weight = [
        first[0] - first[1] * cross / diag[0],
        first[1] - first[0] * cross / diag[1],
    ]
    weight = [jnp.broadcast_to(value, (8, TILE)) for value in weight]

    @pl.when(traded)
    def _():
        for group in range(3):
            drain(gaps_home.at[group_rows(group)], home_recv.at[group])

    def write(index, carry):
        lanes = tile_at(index)
        for source, target in ((home, corrected), (gaps_home, new_residual)):
            target[0, :, :, lanes] = (
                source[pl.ds(0, 3), :, lanes]
                + weight[0] * source[pl.ds(3, 3), :, lanes]
                + weight[1] * source[pl.ds(6, 3), :, lanes]
            )
        return carry

    lax.fori_loop(0, PAIRS, write, 0)

    for unit in range(2):
        for group in range(3):
            wait_pairs(out_send.at[unit, group])
    for group in range(3):
        @pl.when(count == 3)
        def _():
            drain(outgoing.at[group, :, pl.ds(0, 56), pl.ds(0, 3 * TILE)], back_send.at[group])

        @pl.when(count == 2)
        def _():
            drain(outgoing.at[group, :, pl.ds(0, 56), pl.ds(0, 2 * TILE)], back_send.at[group])

    for group in range(3):
        for way, (kind, hop) in enumerate(opposite):
            other, _ = member(kind, hop)
            _, other_count = band(other)
            origin, _ = member(core, hop + 2)
            _, origin_count = band(origin)
            for unit in range(2):
                drain_tiles(
                    slot(passing, unit, group, way, everything, everything),
                    other_count == 3,
                    pass_send.at[unit, group, way],
                )
            drain_tiles(
                slot(passing_back, group, way, everything, everything),
                origin_count == 3,
                pass_back_send.at[group, way],
            )

    @pl.when(traded)
    def _():
        for group in range(3):
            drain(fields.at[group_rows(group)], trade_send.at[group])
            drain(gaps.at[group_rows(group)], home_send.at[group])
        drain(wall_v, trade_send.at[3])

    @pl.when(jnp.logical_or(side == 0, core * side == 1))
    def _():
        for group in range(3):
            drain(fields.at[group_rows(group)], later_send.at[group])

    @pl.when(core * (1 - side) == 1)
    def _():
        for group in range(3):
            drain(home.at[group_rows(group)], home_send.at[3 + group])

    drain(near.at[pl.ds(0, near_count - 1)], sum_send.at[0])
    if far_count > 1:
        drain(far.at[pl.ds(0, far_count - 1)], sum_send.at[1])


def local(nseg, constants, states, tangent_panel, wall_inverse, keep_mask):
    operands = (
        states,
        tangent_panel,
        wall_inverse.reshape(8 * NY, NY),
        keep_mask,
        *[jnp.asarray(value) for value in constants],
    )
    f32 = jnp.float32
    sem = pltpu.SemaphoreType.DMA
    whole = (9, 8, LANES)
    scratch = [
        *[pltpu.VMEM(value.shape, value.dtype) for value in constants],
        pltpu.VMEM((8 * NY, NY), f32),
        pltpu.VMEM((NX, NZ), jnp.int32),
        *[pltpu.VMEM(whole, f32)] * 4,
        pltpu.VMEM((2, 3, 3, 8, 8, 3 * TILE), f32),
        pltpu.VMEM((2, 3, 2, 3, 8, 3 * TILE), f32),
        pltpu.VMEM((3, 12, NX, TILE), f32),
        pltpu.VMEM((3, 3, NX, 3 * TILE), f32),
        pltpu.VMEM((3, 2, 3, 8, 3 * TILE), f32),
        pltpu.VMEM((3, 3, 8, LANES), f32),
        pltpu.VMEM((PAIRS, 2 * PAIRS, 8, TILE), f32),
        *[pltpu.VMEM(whole, f32)] * 6,
        pltpu.VMEM((16, 1, TILE), f32),
        pltpu.VMEM((nseg // 2, 1, TILE), f32),
        sem((11,)),
        sem((4,)),
        sem((4,)),
        sem((2, 3)),
        sem((2, 3)),
        sem((2, 3, 2)),
        sem((2, 3, 2)),
        sem((3,)),
        sem((3,)),
        sem((3, 2)),
        sem((3, 2)),
        sem((3,)),
        sem((3,)),
        sem((6,)),
        sem((3,)),
        sem((2,)),
        sem((2,)),
    ]
    return pl.pallas_call(
        functools.partial(kernel, nseg),
        out_shape=[jax.ShapeDtypeStruct((1, 3, 8, LANES), f32)] * 2,
        in_specs=[pl.BlockSpec(memory_space=pl.ANY)] * len(operands),
        out_specs=[pl.BlockSpec(memory_space=pltpu.VMEM)] * 2,
        scratch_shapes=scratch,
        compiler_params=pltpu.CompilerParams(
            collective_id=0, has_side_effects=True, vmem_limit_bytes=64 * 1024 * 1024
        ),
        name="newton_step",
    )(*operands)


def solution(mesh):
    return jax.shard_map(
        functools.partial(local, mesh.shape["seg"], tables()),
        mesh=mesh,
        in_specs=(
            P("seg", None, "space", None),
            P("seg", None, None, "space", None),
            P("space", None, None),
            P(),
        ),
        out_specs=(P("seg", None, "space", None), P("seg", None, "space", None)),
        check_vma=False,
    )
```

```python
import functools
import math

import jax
import jax.numpy as jnp
import ml_dtypes
import numpy as np
from jax import lax
from jax.experimental import pallas as pl
from jax.experimental.pallas import tpu as pltpu
from jax.sharding import PartitionSpec as P

TIME_STEP = 0.005
VISCOSITY = 0.0025
STREAM_WAVE = 1.0
SPAN_WAVE = 2.0
MESH = pl.DeviceIdType.MESH
NX, NY, NZ = 64, 40, 64
TILE = 128
PAIRS = NY // 2
LANES = NY * NZ


def fourier_basis(length, stretch):
    mode = np.arange(length)[:, None]
    point = np.arange(length)[None, :]
    wave = np.where(mode == length - 1, length // 2, (mode + 1) // 2)
    phase = 2.0 * math.pi / length * (wave * point % length)
    edge = (mode == 0) | (mode == length - 1)
    amplitude = np.where(edge, math.sqrt(1.0 / length), math.sqrt(2.0 / length))
    cosine = (mode % 2 == 1) | (mode == 0)
    basis = amplitude * np.where(cosine, np.cos(phase), np.sin(phase))
    slope = stretch * wave * amplitude * np.where(cosine, -np.sin(phase), np.cos(phase))
    return basis, np.where(edge, 0.0, slope)


def wall_tables(length):
    index = np.arange(1, length + 1)
    height = np.cos(math.pi / (length + 1) * index)
    row, col = height[:, None], height[None, :]
    parity = np.where((index[:, None] + index[None, :]) % 2 == 0, 1.0, -1.0)
    same = index[:, None] == index[None, :]
    spacing = np.where(same, 1.0, row - col)
    return height, np.where(same, -row / (2.0 * (1.0 - row * row)), parity / spacing)


def span_damping(length):
    index = np.arange(length)
    wave = np.where(index == length - 1, length // 2, (index + 1) // 2)
    return 1.0 / (1.0 + TIME_STEP * VISCOSITY * (SPAN_WAVE * wave) ** 2)


def parts(matrix):
    high = matrix.astype(np.float32).astype(ml_dtypes.bfloat16)
    low = (matrix - high.astype(np.float64)).astype(np.float32).astype(ml_dtypes.bfloat16)
    return high, low


def twice(matrix):
    zero = np.zeros_like(matrix)
    return np.block([[matrix, zero], [zero, matrix]])


def tables():
    qx, sx = fourier_basis(NX, STREAM_WAVE)
    qz, sz = fourier_basis(NZ, SPAN_WAVE)
    height, wall = wall_tables(NY)
    high, low = parts(np.concatenate([qx.T, sx.T], axis=0))
    x_forward = np.concatenate([high, high, low], axis=1)
    high, low = parts(qx)
    x_back = np.concatenate([high, high, low], axis=1)
    high, low = parts(np.concatenate([twice(qz), twice(sz)], axis=1))
    z_forward = np.concatenate([high, high, low], axis=0)
    high, low = parts(-TIME_STEP * twice(qz.T))
    z_back = np.concatenate([high, high, low], axis=0)
    derivative = np.zeros((PAIRS, 2 * PAIRS, TILE))
    for half in (0, 1):
        lanes = slice(half * NZ, (half + 1) * NZ)
        derivative[:, 0::2, lanes] = wall[half::2, half::2][:, :, None]
        derivative[:, 1::2, lanes] = wall[half::2, 1 - half :: 2][:, :, None]
    heights = np.repeat(height.reshape(PAIRS, 1, 2), NZ, axis=2)
    damping = np.tile(span_damping(NZ), 2)[None, :]
    single = [value.astype(np.float32) for value in (derivative, heights, damping)]
    return (x_forward, x_back, z_forward, z_back, *single)


def band(place):
    row, side = lax.rem(place, 4), lax.div(place, 4)
    odd = lax.rem(row, 2)
    count = 3 - lax.rem(row + side, 2)
    return 5 * row + side * (3 - odd), count


def tile_at(index, tiles=1):
    return pl.ds(pl.multiple_of(index * TILE, TILE), tiles * TILE)


def split(value):
    high = value.astype(jnp.bfloat16)
    low = (value - high.astype(jnp.float32)).astype(jnp.bfloat16)
    return high, low


def stacked(value, axis):
    high, low = split(value)
    return jnp.concatenate([high, low, high], axis=axis)


def mul(a, b):
    return jnp.dot(a, b, preferred_element_type=jnp.float32)


def kernel(
    nseg,
    states,
    panel,
    wall,
    mask,
    x_forward_in,
    x_back_in,
    z_forward_in,
    z_back_in,
    derivative_in,
    heights_in,
    damping_in,
    gaps_home,
    message_out,
    x_forward,
    x_back,
    z_forward,
    z_back,
    derivative,
    heights,
    damping,
    wall_v,
    mask_v,
    fields,
    swapped,
    slopes,
    got,
    passing,
    flow,
    outgoing,
    passing_back,
    returned,
    solve,
    forced,
    turned,
    ends,
    later,
    gaps,
    in_sem,
    trade_send,
    trade_recv,
    out_send,
    out_recv,
    pass_send,
    pass_recv,
    back_send,
    back_recv,
    pass_back_send,
    pass_back_recv,
    later_send,
    later_recv,
    home_send,
    home_recv,
):
    seg = lax.axis_index("seg")
    space = lax.axis_index("space")
    core = lax.rem(seg, 2)
    side = lax.div(space, 4)
    row = lax.rem(space, 4)
    base = seg - core
    near_count = 16
    near_me = core * 8 + space
    place = core * 4 + row
    traded = core + side == 1
    trader = (base + side, place)
    first_pair, count = band(place)

    def near_device(step):
        other = lax.rem(near_me + step, near_count)
        return (base + lax.div(other, 8), lax.rem(other, 8))

    def member(kind, hop):
        where = lax.rem(row + hop + 4, 4)
        return kind * 4 + where, (base + kind, side * 4 + where)

    next_pair = lax.rem(seg + 2 * side - 2 * (1 - side) + nseg, nseg)
    across = (next_pair, space + 4 * (1 - side) - 4 * side)

    barrier = pltpu.get_barrier_semaphore()
    for step in range(1, near_count):
        pl.semaphore_signal(barrier, inc=1, device_id=near_device(step), device_id_type=MESH)
    pl.semaphore_signal(barrier, inc=1, device_id=across, device_id_type=MESH)

    own = [states.at[0], panel.at[0, 0], panel.at[0, 1]]

    def group_rows(group):
        return pl.ds(3 * group, 3)

    loads = [
        (derivative_in, derivative),
        (mask, mask_v),
        (x_forward_in, x_forward),
        (z_forward_in, z_forward),
        (x_back_in, x_back),
        (z_back_in, z_back),
        (heights_in, heights),
        (damping_in, damping),
    ]
    loads = [
        pltpu.make_async_copy(src, dst, in_sem.at[index])
        for index, (src, dst) in enumerate(loads)
    ]
    begins = [(wall, wall_v)] + [(own[group], fields.at[group_rows(group)]) for group in range(3)]

    @pl.when(jnp.logical_not(traded))
    def _():
        for index, (src, dst) in enumerate(begins):
            pltpu.make_async_copy(src, dst, trade_recv.at[index]).start()

    for load in loads:
        load.start()
    pl.semaphore_wait(barrier, near_count)

    def send(src, dst, send_sem, recv_sem, device):
        pltpu.make_async_remote_copy(
            src_ref=src,
            dst_ref=dst,
            send_sem=send_sem,
            recv_sem=recv_sem,
            device_id=device,
            device_id_type=MESH,
        ).start()

    def send_tiles(src, dst, three, send_sem, recv_sem, device):
        send(src(0, 2), dst(0, 2), send_sem, recv_sem, device)

        @pl.when(three)
        def _():
            send(src(2, 1), dst(2, 1), send_sem, recv_sem, device)

    @pl.when(traded)
    def _():
        for index, (src, dst) in enumerate(begins):
            send(src, dst, trade_send.at[index], trade_recv.at[index], trader)

    def slot(ref, *index):
        return lambda start, tiles: ref.at[(*index, pl.ds(start * TILE, tiles * TILE))]

    def band_of(ref, first, *index):
        return lambda start, tiles: ref.at[(*index, tile_at(first + start, tiles))]

    everything = slice(None)
    direct = [(1 - core, 0), (0, 1), (1, 1), (0, 3), (1, 3)]
    opposite = [(0, 1), (1, 3)]

    def send_heights(unit, group, source):
        sems = out_send.at[unit, group]
        for way, (kind, hop) in enumerate(opposite):
            other, _ = member(kind, 2)
            _, relay = member(core, hop)
            other_first, other_count = band(other)
            send_tiles(
                band_of(source, other_first, everything, everything),
                slot(passing, unit, group, way, everything, everything),
                other_count == 3,
                sems,
                pass_recv.at[unit, group, way],
                relay,
            )
        for kind, hop in direct:
            other, device = member(kind, hop)
            other_first, other_count = band(other)
            send_tiles(
                band_of(source, other_first, everything, everything),
                slot(got, unit, group, everything, place, everything),
                other_count == 3,
                sems,
                out_recv.at[unit, group],
                device,
            )

    def drain_tiles(ref, three, sem):
        @pl.when(three)
        def _():
            drain(ref(0, 3), sem)

        @pl.when(jnp.logical_not(three))
        def _():
            drain(ref(0, 2), sem)

    def pass_heights(unit, group):
        for way, (kind, hop) in enumerate(opposite):
            origin, _ = member(core, hop + 2)
            other, device = member(kind, hop)
            _, other_count = band(other)
            held = slot(passing, unit, group, way, everything, everything)
            drain_tiles(held, other_count == 3, pass_recv.at[unit, group, way])
            send_tiles(
                held,
                slot(got, unit, group, everything, origin, everything),
                other_count == 3,
                pass_send.at[unit, group, way],
                out_recv.at[unit, group],
                device,
            )

    def keep_heights(unit, group, source):
        got[unit, group, :, place, :, pl.ds(0, 2 * TILE)] = source[
            group_rows(group), :, tile_at(first_pair, 2)
        ]

        @pl.when(count == 3)
        def _():
            got[unit, group, :, place, :, pl.ds(2 * TILE, TILE)] = source[
                group_rows(group), :, tile_at(first_pair + 2)
            ]

    def drain(ref, sem):
        pltpu.make_async_copy(ref, ref, sem).wait()

    def wait_heights(unit, group):
        @pl.when(count == 3)
        def _():
            drain(
                got.at[unit, group, :, pl.ds(0, 7), :, pl.ds(0, 3 * TILE)],
                out_recv.at[unit, group],
            )

        @pl.when(count == 2)
        def _():
            drain(
                got.at[unit, group, :, pl.ds(0, 7), :, pl.ds(0, 2 * TILE)],
                out_recv.at[unit, group],
            )

    def wait_pairs(sem):
        @pl.when(count == 3)
        def _():
            drain(returned.at[0, :, :, pl.ds(0, (PAIRS - 3) * TILE)], sem)

        @pl.when(count == 2)
        def _():
            drain(returned.at[0, :, :, pl.ds(0, (PAIRS - 2) * TILE)], sem)

    def across_heights(group, source, other, coefficient, target):
        rows = pl.ds(3 * group, 3)

        def step(index, carry):
            sums = [jnp.zeros((3, 8, TILE), jnp.float32) for _ in range(2)]
            for pair in range(PAIRS):
                lanes = pl.ds(pair * TILE, TILE)
                straight, turned_pair = source[rows, :, lanes], other[rows, :, lanes]
                for which in range(2):
                    sums[which] += coefficient(2 * index + which, 2 * pair) * straight
                    sums[which] += coefficient(2 * index + which, 2 * pair + 1) * turned_pair
            target[rows, :, tile_at(2 * index)] = sums[0]
            target[rows, :, tile_at(2 * index + 1)] = sums[1]
            return carry

        lax.fori_loop(0, PAIRS // 2, step, 0)

    def turn(group, source, target):
        rows = pl.ds(3 * group, 3)
        for pair in range(PAIRS):
            lanes = pl.ds(pair * TILE, TILE)
            target[rows, :, lanes] = pltpu.roll(source[rows, :, lanes], NZ, 2)

    def begin(group):
        drain(fields.at[group_rows(group)], trade_recv.at[1 + group])
        send_heights(0, group, fields.at[group_rows(group)])
        keep_heights(0, group, fields)

    def differentiate(group):
        turn(group, fields, swapped)
        across_heights(
            group,
            fields,
            swapped,
            lambda pair, row: derivative[pair, pl.ds(row, 1), :],
            slopes,
        )

    def send_slopes(group):
        send_heights(1, group, slopes.at[group_rows(group)])
        keep_heights(1, group, slopes)

    def send_start(sources, device):
        for group in range(3):
            send(
                sources[group],
                later.at[group_rows(group)],
                later_send.at[group],
                later_recv.at[group],
                device,
            )

    def shift():
        mine = [fields.at[group_rows(group)] for group in range(3)]

        @pl.when(side == 0)
        def _():
            send_start(mine, across)

        @pl.when(core * side == 1)
        def _():
            send_start(mine, (seg, space - 4))

        @pl.when(core * (1 - side) == 1)
        def _():
            for group in range(3):
                send(
                    own[group],
                    later.at[group_rows(group)],
                    home_send.at[3 + group],
                    later_recv.at[group],
                    (seg - 1, space),
                )

    lane = lax.broadcasted_iota(jnp.int32, (8, TILE), 1)
    low_half = lane < NZ

    def solve_rows(pair, carry):
        even = wall_v[pl.ds(2 * pair, 8, stride=NY), :]
        odd = wall_v[pl.ds(2 * pair + 1, 8, stride=NY), :]

        def spread(value, column):
            return jnp.broadcast_to(value[:, column : column + 1], (8, TILE))

        for other in range(PAIRS):
            solve[pair, 2 * other] = jnp.where(
                low_half, spread(even, 2 * other), spread(odd, 2 * other + 1)
            )
            solve[pair, 2 * other + 1] = jnp.where(
                low_half, spread(even, 2 * other + 1), spread(odd, 2 * other)
            )
        return carry

    def kept():
        rows = mask_v[pl.ds(pl.multiple_of(place * 8, 8), 8), :].astype(jnp.float32)
        return jnp.concatenate([rows, rows], axis=1) * damping[...]

    def transform(group):
        wait_heights(0, group)
        wait_heights(1, group)

        def modes(unit):
            value = got[unit, group].reshape(3, NX, 3 * TILE)
            return stacked(jnp.concatenate([value[0], value[1], value[2]], axis=1), 0)

        def by_rows(value):
            return [value[:, c * TILE : (c + 1) * TILE] for c in range(9)]

        in_x = mul(x_forward[...], modes(0))
        in_x_wall = mul(x_forward[pl.ds(0, NX), :], modes(1))
        plain = jnp.concatenate(by_rows(in_x[:NX]), axis=0)
        rest = jnp.concatenate(by_rows(in_x[NX:]) + by_rows(in_x_wall), axis=0)
        pair = mul(stacked(plain, 1), z_forward[...])
        single = mul(stacked(rest, 1), z_forward[:, pl.ds(0, TILE)])
        total = [None] * 9
        for index in range(3):

            def field(value, c):
                row = (3 * c + index) * NX
                return value[row : row + NX]

            physical = [field(pair[:, :TILE], c) for c in range(3)]
            span = [field(pair[:, TILE:], c) for c in range(3)]
            stream = [field(single, c) for c in range(3)]
            slope = [field(single, c + 3) for c in range(3)]
            if group == 0:
                for c in range(3):
                    flow[index, c] = physical[c]
                    flow[index, 3 + c] = stream[c]
                    flow[index, 6 + c] = slope[c]
                    flow[index, 9 + c] = span[c]
                u, v, w = physical
            else:
                u, v, w = (flow[index, c] for c in range(3))
            u = u + heights[lax.min(first_pair + index, PAIRS - 1)]
            for c in range(3):
                value = u * stream[c] + v * slope[c] + w * span[c]
                if group > 0:
                    value += (
                        physical[0] * flow[index, 3 + c]
                        + physical[1] * flow[index, 6 + c]
                        + physical[2] * flow[index, 9 + c]
                    )
                if c == 0:
                    value += physical[1]
                total[3 * c + index] = value
        in_k = mul(stacked(jnp.concatenate(total, axis=0), 1), z_back[...])
        in_k = jnp.concatenate([in_k[c * NX : (c + 1) * NX] for c in range(9)], axis=1)
        in_m = mul(x_back[...], stacked(in_k, 0))
        for c in range(3):
            outgoing[group, c] = in_m[:, 3 * c * TILE : 3 * (c + 1) * TILE]

        def rows_of(other):
            return pl.ds(pl.multiple_of(other * 8, 8), 8)

        for way, (kind, hop) in enumerate(opposite):
            other, _ = member(kind, 2)
            _, relay = member(core, hop)
            send_tiles(
                slot(outgoing, group, everything, rows_of(other)),
                slot(passing_back, group, way, everything, everything),
                count == 3,
                back_send.at[group],
                pass_back_recv.at[group, way],
                relay,
            )
        for kind, hop in direct:
            other, device = member(kind, hop)
            send_tiles(
                slot(outgoing, group, everything, rows_of(other)),
                band_of(returned, first_pair, group, everything, everything),
                count == 3,
                back_send.at[group],
                back_recv.at[group],
                device,
            )

        mine = rows_of(place)
        returned[group, :, :, tile_at(first_pair, 2)] = outgoing[
            group, :, mine, pl.ds(0, 2 * TILE)
        ]

        @pl.when(count == 3)
        def _():
            returned[group, :, :, tile_at(first_pair + 2)] = outgoing[
                group, :, mine, pl.ds(2 * TILE, TILE)
            ]

    def pass_back(group):
        for way, (kind, hop) in enumerate(opposite):
            origin, _ = member(core, hop + 2)
            _, device = member(kind, hop)
            origin_first, origin_count = band(origin)
            held = slot(passing_back, group, way, everything, everything)
            drain_tiles(held, origin_count == 3, pass_back_recv.at[group, way])
            send_tiles(
                held,
                band_of(returned, origin_first, group, everything, everything),
                origin_count == 3,
                pass_back_send.at[group, way],
                back_recv.at[group],
                device,
            )

    def finish(group, keep):
        wait_pairs(back_recv.at[group])
        rows = group_rows(group)
        for pair in range(PAIRS):
            lanes = pl.ds(pair * TILE, TILE)
            value = keep * (fields[rows, :, lanes] + returned[group, :, :, lanes])
            forced[rows, :, lanes] = value
            turned[rows, :, lanes] = pltpu.roll(value, NZ, 2)
        across_heights(
            group, forced, turned, lambda pair, row: solve[pair, row], ends
        )
        drain(later.at[rows], later_recv.at[group])
        gap = ends[rows] - later[rows]
        gaps[rows] = gap

        @pl.when(traded)
        def _():
            send(
                gaps.at[rows],
                gaps_home.at[rows],
                home_send.at[group],
                home_recv.at[group],
                trader,
            )

        @pl.when(jnp.logical_not(traded))
        def _():
            gaps_home[rows] = gap

    drain(wall_v, trade_recv.at[0])
    lax.fori_loop(0, PAIRS, solve_rows, 0)
    begin(0)
    loads[0].wait()
    differentiate(0)
    send_slopes(0)
    pass_heights(0, 0)
    begin(1)
    differentiate(1)
    pass_heights(1, 0)
    send_slopes(1)
    pass_heights(0, 1)
    begin(2)
    differentiate(2)
    pass_heights(1, 1)
    send_slopes(2)
    shift()
    for load in loads[1:]:
        load.wait()
    keep = kept()
    pass_heights(0, 2)
    transform(0)
    pass_heights(1, 2)
    transform(1)
    pass_back(0)
    transform(2)
    pass_back(1)
    finish(0, keep)
    pass_back(2)
    finish(1, keep)
    finish(2, keep)

    def products(index, sums):
        lanes = tile_at(index)
        start = [fields[group_rows(g), :, lanes] for g in range(3)]
        gap = [gaps[group_rows(g), :, lanes] for g in range(3)]
        drift = ends[group_rows(0), :, lanes] - start[0]
        terms = [
            drift * start[1],
            drift * start[2],
            gap[1] * gap[1],
            gap[2] * gap[2],
            gap[1] * gap[0],
            gap[2] * gap[0],
            gap[1] * gap[2],
        ]
        return tuple(s + t[0] + t[1] + t[2] for s, t in zip(sums, terms))

    sums = lax.fori_loop(
        0, PAIRS, products, tuple(jnp.zeros((8, TILE), jnp.float32) for _ in range(7))
    )
    column = lax.broadcasted_iota(jnp.int32, (1, TILE), 1)
    message = jnp.zeros((1, TILE), jnp.float32)
    for index, value in enumerate(sums):
        total = jnp.sum(jnp.sum(value, axis=0, keepdims=True), axis=1, keepdims=True)
        message = jnp.where(column == index, total, message)

    message_out[...] = message

    @pl.when(traded)
    def _():
        for group in range(3):
            drain(gaps_home.at[group_rows(group)], home_recv.at[group])

    for unit in range(2):
        for group in range(3):
            wait_pairs(out_send.at[unit, group])
    for group in range(3):
        @pl.when(count == 3)
        def _():
            drain(outgoing.at[group, :, pl.ds(0, 56), pl.ds(0, 3 * TILE)], back_send.at[group])

        @pl.when(count == 2)
        def _():
            drain(outgoing.at[group, :, pl.ds(0, 56), pl.ds(0, 2 * TILE)], back_send.at[group])

    for group in range(3):
        for way, (kind, hop) in enumerate(opposite):
            other, _ = member(kind, hop)
            _, other_count = band(other)
            origin, _ = member(core, hop + 2)
            _, origin_count = band(origin)
            for unit in range(2):
                drain_tiles(
                    slot(passing, unit, group, way, everything, everything),
                    other_count == 3,
                    pass_send.at[unit, group, way],
                )
            drain_tiles(
                slot(passing_back, group, way, everything, everything),
                origin_count == 3,
                pass_back_send.at[group, way],
            )

    @pl.when(traded)
    def _():
        for group in range(3):
            drain(fields.at[group_rows(group)], trade_send.at[1 + group])
            drain(gaps.at[group_rows(group)], home_send.at[group])
        drain(wall_v, trade_send.at[0])

    @pl.when(jnp.logical_or(side == 0, core * side == 1))
    def _():
        for group in range(3):
            drain(fields.at[group_rows(group)], later_send.at[group])

    @pl.when(core * (1 - side) == 1)
    def _():
        for group in range(3):
            drain(fields.at[group_rows(group)], home_send.at[3 + group])


def sum_kernel(nseg, message, weights, near, far, sum_send, sum_recv):
    seg = lax.axis_index("seg")
    space = lax.axis_index("space")
    core = lax.rem(seg, 2)
    chip_pair = lax.div(seg, 2)
    near_count, far_count = 16, nseg // 2
    near_me = core * 8 + space

    def near_device(step):
        other = lax.rem(near_me + step, near_count)
        return (seg - core + lax.div(other, 8), lax.rem(other, 8))

    def far_device(step):
        return (2 * lax.rem(chip_pair + step, far_count) + core, space)

    barrier = pltpu.get_barrier_semaphore()
    for step in range(1, near_count):
        pl.semaphore_signal(barrier, inc=1, device_id=near_device(step), device_id_type=MESH)
    for step in range(1, far_count):
        pl.semaphore_signal(barrier, inc=1, device_id=far_device(step), device_id_type=MESH)
    pl.semaphore_wait(barrier, near_count + far_count - 2)

    def drain(ref, sem):
        pltpu.make_async_copy(ref, ref, sem).wait()

    def exchange(which, slots, me, size, device, value):
        slots[me] = value
        for step in range(1, size):
            pltpu.make_async_remote_copy(
                src_ref=slots.at[me],
                dst_ref=slots.at[me],
                send_sem=sum_send.at[which],
                recv_sem=sum_recv.at[which],
                device_id=device(step),
                device_id_type=MESH,
            ).start()
        if size > 1:
            drain(slots.at[pl.ds(0, size - 1)], sum_recv.at[which])
        return jnp.sum(slots[...], axis=0)

    total = exchange(0, near, near_me, near_count, near_device, message[...])
    total = exchange(1, far, chip_pair, far_count, far_device, total)

    def number(index):
        return total[:, index : index + 1]

    root = 1.0 / math.sqrt(nseg * 3 * NX * LANES)
    border = [number(0) * root, number(1) * root]
    diag = [number(2) + border[0] * border[0], number(3) + border[1] * border[1]]
    first = [-number(4) / diag[0], -number(5) / diag[1]]
    cross = number(6) + border[0] * border[1]
    weights[pl.ds(0, 1), :] = jnp.broadcast_to(first[0] - first[1] * cross / diag[0], (1, TILE))
    weights[pl.ds(1, 1), :] = jnp.broadcast_to(first[1] - first[0] * cross / diag[1], (1, TILE))
    drain(near.at[pl.ds(0, near_count - 1)], sum_send.at[0])
    if far_count > 1:
        drain(far.at[pl.ds(0, far_count - 1)], sum_send.at[1])


def final_kernel(states, panel, gaps, weights, corrected, new_residual):
    a = jnp.broadcast_to(weights[pl.ds(0, 1), :], (8, TILE))
    b = jnp.broadcast_to(weights[pl.ds(1, 1), :], (8, TILE))
    for pair in range(PAIRS):
        lanes = pl.ds(pair * TILE, TILE)
        corrected[0, :, :, lanes] = (
            states[0, :, :, lanes] + a * panel[0, 0, :, :, lanes] + b * panel[0, 1, :, :, lanes]
        )
        new_residual[0, :, :, lanes] = (
            gaps[pl.ds(0, 3), :, lanes]
            + a * gaps[pl.ds(3, 3), :, lanes]
            + b * gaps[pl.ds(6, 3), :, lanes]
        )


def local(nseg, constants, states, tangent_panel, wall_inverse, keep_mask):
    operands = (
        states,
        tangent_panel,
        wall_inverse.reshape(8 * NY, NY),
        keep_mask,
        *[jnp.asarray(value) for value in constants],
    )
    f32 = jnp.float32
    sem = pltpu.SemaphoreType.DMA
    whole = (9, 8, LANES)
    scratch = [
        *[pltpu.VMEM(value.shape, value.dtype) for value in constants],
        pltpu.VMEM((8 * NY, NY), f32),
        pltpu.VMEM((NX, NZ), jnp.int32),
        *[pltpu.VMEM(whole, f32)] * 3,
        pltpu.VMEM((2, 3, 3, 8, 8, 3 * TILE), f32),
        pltpu.VMEM((2, 3, 2, 3, 8, 3 * TILE), f32),
        pltpu.VMEM((3, 12, NX, TILE), f32),
        pltpu.VMEM((3, 3, NX, 3 * TILE), f32),
        pltpu.VMEM((3, 2, 3, 8, 3 * TILE), f32),
        pltpu.VMEM((3, 3, 8, LANES), f32),
        pltpu.VMEM((PAIRS, 2 * PAIRS, 8, TILE), f32),
        *[pltpu.VMEM(whole, f32)] * 5,
        sem((8,)),
        sem((4,)),
        sem((4,)),
        sem((2, 3)),
        sem((2, 3)),
        sem((2, 3, 2)),
        sem((2, 3, 2)),
        sem((3,)),
        sem((3,)),
        sem((3, 2)),
        sem((3, 2)),
        sem((3,)),
        sem((3,)),
        sem((6,)),
        sem((3,)),
    ]
    vmem = pl.BlockSpec(memory_space=pltpu.VMEM)
    gaps, message = pl.pallas_call(
        functools.partial(kernel, nseg),
        out_shape=[
            jax.ShapeDtypeStruct(whole, f32),
            jax.ShapeDtypeStruct((1, TILE), f32),
        ],
        in_specs=[pl.BlockSpec(memory_space=pl.ANY)] * len(operands),
        out_specs=[vmem, vmem],
        scratch_shapes=scratch,
        compiler_params=pltpu.CompilerParams(
            collective_id=0, has_side_effects=True, vmem_limit_bytes=64 * 1024 * 1024
        ),
        name="newton_step",
    )(*operands)
    weights = pl.pallas_call(
        functools.partial(sum_kernel, nseg),
        out_shape=jax.ShapeDtypeStruct((2, TILE), f32),
        in_specs=[vmem],
        out_specs=vmem,
        scratch_shapes=[
            pltpu.VMEM((16, 1, TILE), f32),
            pltpu.VMEM((nseg // 2, 1, TILE), f32),
            sem((2,)),
            sem((2,)),
        ],
        compiler_params=pltpu.CompilerParams(
            collective_id=1, has_side_effects=True, vmem_limit_bytes=64 * 1024 * 1024
        ),
        name="newton_sums",
    )(message)
    result = jax.ShapeDtypeStruct((1, 3, 8, LANES), f32)
    return pl.pallas_call(
        final_kernel,
        out_shape=[result, result],
        in_specs=[vmem] * 4,
        out_specs=[vmem, vmem],
        compiler_params=pltpu.CompilerParams(vmem_limit_bytes=64 * 1024 * 1024),
        name="newton_final",
    )(states, tangent_panel, gaps, weights)


def solution(mesh):
    return jax.shard_map(
        functools.partial(local, mesh.shape["seg"], tables()),
        mesh=mesh,
        in_specs=(
            P("seg", None, "space", None),
            P("seg", None, None, "space", None),
            P("space", None, None),
            P(),
        ),
        out_specs=(P("seg", None, "space", None), P("seg", None, "space", None)),
        check_vma=False,
    )
```

```python
import functools
import math

import jax
import jax.numpy as jnp
import ml_dtypes
import numpy as np
from jax import lax
from jax.experimental import pallas as pl
from jax.experimental.pallas import tpu as pltpu
from jax.sharding import PartitionSpec as P

TIME_STEP = 0.005
VISCOSITY = 0.0025
STREAM_WAVE = 1.0
SPAN_WAVE = 2.0
MESH = pl.DeviceIdType.MESH
NX, NY, NZ = 64, 40, 64
TILE = 128
PAIRS = NY // 2
LANES = NY * NZ


def fourier_basis(length, stretch):
    mode = np.arange(length)[:, None]
    point = np.arange(length)[None, :]
    wave = np.where(mode == length - 1, length // 2, (mode + 1) // 2)
    phase = 2.0 * math.pi / length * (wave * point % length)
    edge = (mode == 0) | (mode == length - 1)
    amplitude = np.where(edge, math.sqrt(1.0 / length), math.sqrt(2.0 / length))
    cosine = (mode % 2 == 1) | (mode == 0)
    basis = amplitude * np.where(cosine, np.cos(phase), np.sin(phase))
    slope = stretch * wave * amplitude * np.where(cosine, -np.sin(phase), np.cos(phase))
    return basis, np.where(edge, 0.0, slope)


def wall_tables(length):
    index = np.arange(1, length + 1)
    height = np.cos(math.pi / (length + 1) * index)
    row, col = height[:, None], height[None, :]
    parity = np.where((index[:, None] + index[None, :]) % 2 == 0, 1.0, -1.0)
    same = index[:, None] == index[None, :]
    spacing = np.where(same, 1.0, row - col)
    return height, np.where(same, -row / (2.0 * (1.0 - row * row)), parity / spacing)


def span_damping(length):
    index = np.arange(length)
    wave = np.where(index == length - 1, length // 2, (index + 1) // 2)
    return 1.0 / (1.0 + TIME_STEP * VISCOSITY * (SPAN_WAVE * wave) ** 2)


def parts(matrix):
    high = matrix.astype(np.float32).astype(ml_dtypes.bfloat16)
    low = (matrix - high.astype(np.float64)).astype(np.float32).astype(ml_dtypes.bfloat16)
    return high, low


def twice(matrix):
    zero = np.zeros_like(matrix)
    return np.block([[matrix, zero], [zero, matrix]])


def tables():
    qx, sx = fourier_basis(NX, STREAM_WAVE)
    qz, sz = fourier_basis(NZ, SPAN_WAVE)
    height, wall = wall_tables(NY)
    high, low = parts(np.concatenate([qx.T, sx.T], axis=0))
    x_forward = np.concatenate([high, high, low], axis=1)
    high, low = parts(qx)
    x_back = np.concatenate([high, high, low], axis=1)
    high, low = parts(np.concatenate([twice(qz), twice(sz)], axis=1))
    z_forward = np.concatenate([high, high, low], axis=0)
    high, low = parts(-TIME_STEP * twice(qz.T))
    z_back = np.concatenate([high, high, low], axis=0)
    derivative = np.zeros((PAIRS, 2 * PAIRS, TILE))
    for half in (0, 1):
        lanes = slice(half * NZ, (half + 1) * NZ)
        derivative[:, 0::2, lanes] = wall[half::2, half::2][:, :, None]
        derivative[:, 1::2, lanes] = wall[half::2, 1 - half :: 2][:, :, None]
    heights = np.repeat(height.reshape(PAIRS, 1, 2), NZ, axis=2)
    damping = np.tile(span_damping(NZ), 2)[None, :]
    single = [value.astype(np.float32) for value in (derivative, heights, damping)]
    return (x_forward, x_back, z_forward, z_back, *single)


def band(place):
    row, side = lax.rem(place, 4), lax.div(place, 4)
    odd = lax.rem(row, 2)
    count = 3 - lax.rem(row + side, 2)
    return 5 * row + side * (3 - odd), count


def tile_at(index, tiles=1):
    return pl.ds(pl.multiple_of(index * TILE, TILE), tiles * TILE)


def split(value):
    high = value.astype(jnp.bfloat16)
    low = (value - high.astype(jnp.float32)).astype(jnp.bfloat16)
    return high, low


def stacked(value, axis):
    high, low = split(value)
    return jnp.concatenate([high, low, high], axis=axis)


def mul(a, b):
    return jnp.dot(a, b, preferred_element_type=jnp.float32)


def kernel(
    nseg,
    states,
    panel,
    wall,
    mask,
    x_forward_in,
    x_back_in,
    z_forward_in,
    z_back_in,
    derivative_in,
    heights_in,
    damping_in,
    corrected,
    new_residual,
    x_forward,
    x_back,
    z_forward,
    z_back,
    derivative,
    heights,
    damping,
    wall_v,
    mask_v,
    home,
    pack,
    swapped,
    got,
    passing,
    flow,
    outgoing,
    passing_back,
    returned,
    solve,
    forced,
    turned,
    ends,
    later,
    gaps,
    gaps_home,
    ring_sums,
    side_sums,
    far_sums,
    in_sem,
    trade_send,
    trade_recv,
    out_send,
    out_recv,
    pass_send,
    pass_recv,
    back_send,
    back_recv,
    pass_back_send,
    pass_back_recv,
    later_send,
    later_recv,
    home_send,
    home_recv,
    sum_send,
    sum_recv,
):
    seg = lax.axis_index("seg")
    space = lax.axis_index("space")
    core = lax.rem(seg, 2)
    side = lax.div(space, 4)
    row = lax.rem(space, 4)
    base = seg - core
    chip_pair = lax.div(seg, 2)
    low_count = min(4, nseg // 2)
    far_count = nseg // 2 // low_count
    side_count = 2 * low_count
    low, high = lax.rem(chip_pair, low_count), lax.div(chip_pair, low_count)
    side_me = side * low_count + low
    fields, slopes = pack.at[0], pack.at[1]
    place = core * 4 + row
    traded = core + side == 1
    trader = (base + side, place)
    first_pair, count = band(place)

    def member(kind, hop):
        where = lax.rem(row + hop + 4, 4)
        return kind * 4 + where, (base + kind, side * 4 + where)

    next_pair = lax.rem(seg + 2 * side - 2 * (1 - side) + nseg, nseg)
    across = (next_pair, space + 4 * (1 - side) - 4 * side)

    def ring_device(step):
        other = lax.rem(place + step, 8)
        return (base + lax.div(other, 4), side * 4 + lax.rem(other, 4))

    def side_device(step):
        other = lax.rem(side_me + step, side_count)
        pair = high * low_count + lax.rem(other, low_count)
        return (2 * pair + core, lax.div(other, low_count) * 4 + row)

    def far_device(step):
        return (2 * (lax.rem(high + step, far_count) * low_count + low) + core, space)

    rounds = [(8, ring_device), (side_count, side_device), (far_count, far_device)]
    barrier = pltpu.get_barrier_semaphore()

    def greet(device):
        pl.semaphore_signal(barrier, inc=1, device_id=device, device_id_type=MESH)

    @pl.when(traded)
    def _():
        greet(trader)

    for size, device in rounds:
        for step in range(1, size):
            greet(device(step))
    greet(across)

    own = [states.at[0], panel.at[0, 0], panel.at[0, 1]]

    def group_rows(group):
        return pl.ds(3 * group, 3)

    loads = [
        (derivative_in, derivative),
        (mask, mask_v),
        (x_forward_in, x_forward),
        (z_forward_in, z_forward),
        (x_back_in, x_back),
        (z_back_in, z_back),
        (heights_in, heights),
        (damping_in, damping),
        *[(own[group], home.at[group_rows(group)]) for group in range(3)],
    ]
    loads = [
        pltpu.make_async_copy(src, dst, in_sem.at[index])
        for index, (src, dst) in enumerate(loads)
    ]
    begins = [(wall, wall_v)] + [(own[group], fields.at[group_rows(group)]) for group in range(3)]

    @pl.when(jnp.logical_not(traded))
    def _():
        for index, (src, dst) in enumerate(begins):
            pltpu.make_async_copy(src, dst, trade_recv.at[index]).start()

    for load in loads:
        load.start()
    greetings = sum(size - 1 for size, _ in rounds) + 1

    @pl.when(traded)
    def _():
        pl.semaphore_wait(barrier, greetings + 1)

    @pl.when(jnp.logical_not(traded))
    def _():
        pl.semaphore_wait(barrier, greetings)


    def send(src, dst, send_sem, recv_sem, device):
        pltpu.make_async_remote_copy(
            src_ref=src,
            dst_ref=dst,
            send_sem=send_sem,
            recv_sem=recv_sem,
            device_id=device,
            device_id_type=MESH,
        ).start()

    def send_tiles(src, dst, three, send_sem, recv_sem, device):
        @pl.when(three)
        def _():
            send(src(3), dst(3), send_sem, recv_sem, device)

        @pl.when(jnp.logical_not(three))
        def _():
            send(src(2), dst(2), send_sem, recv_sem, device)

    @pl.when(traded)
    def _():
        for index, (src, dst) in enumerate(begins):
            send(src, dst, trade_send.at[index], trade_recv.at[index], trader)

    def slot(ref, *index):
        return lambda tiles: ref.at[(*index, pl.ds(0, tiles * TILE))]

    def band_of(ref, first, *index):
        return lambda tiles: ref.at[(*index, tile_at(first, tiles))]

    everything = slice(None)
    direct = [(1 - core, 0), (0, 1), (1, 1), (0, 3), (1, 3)]
    opposite = [(0, 1), (1, 3)]

    def send_heights(group):
        source = (pack, everything, group_rows(group), everything)
        for way, (kind, hop) in enumerate(opposite):
            other, _ = member(kind, 2)
            _, relay = member(core, hop)
            other_first, other_count = band(other)
            send_tiles(
                band_of(source[0], other_first, *source[1:]),
                slot(passing, group, way, everything, everything, everything),
                other_count == 3,
                out_send.at[group],
                pass_recv.at[group, way],
                relay,
            )
        for kind, hop in direct:
            other, device = member(kind, hop)
            other_first, other_count = band(other)
            send_tiles(
                band_of(source[0], other_first, *source[1:]),
                slot(got, group, everything, everything, place, everything),
                other_count == 3,
                out_send.at[group],
                out_recv.at[group],
                device,
            )

    def drain_tiles(ref, three, sem):
        @pl.when(three)
        def _():
            drain(ref(3), sem)

        @pl.when(jnp.logical_not(three))
        def _():
            drain(ref(2), sem)

    def pass_heights(group):
        for way, (kind, hop) in enumerate(opposite):
            origin, _ = member(core, hop + 2)
            other, device = member(kind, hop)
            _, other_count = band(other)
            held = slot(passing, group, way, everything, everything, everything)
            drain_tiles(held, other_count == 3, pass_recv.at[group, way])
            send_tiles(
                held,
                slot(got, group, everything, everything, origin, everything),
                other_count == 3,
                pass_send.at[group, way],
                out_recv.at[group],
                device,
            )

    def keep_heights(group):
        for unit in range(2):
            got[group, unit, :, place, :, pl.ds(0, 2 * TILE)] = pack[
                unit, group_rows(group), :, tile_at(first_pair, 2)
            ]

            @pl.when(count == 3)
            def _():
                got[group, unit, :, place, :, pl.ds(2 * TILE, TILE)] = pack[
                    unit, group_rows(group), :, tile_at(first_pair + 2)
                ]

    def drain(ref, sem):
        pltpu.make_async_copy(ref, ref, sem).wait()

    def wait_heights(group):
        arrived = slot(got, group, everything, everything, pl.ds(0, 7), everything)
        drain_tiles(arrived, count == 3, out_recv.at[group])

    def wait_pairs(ref, sem):
        @pl.when(count == 3)
        def _():
            drain(ref.at[..., pl.ds(0, (PAIRS - 3) * TILE)], sem)

        @pl.when(count == 2)
        def _():
            drain(ref.at[..., pl.ds(0, (PAIRS - 2) * TILE)], sem)

    def across_heights(group, source, other, coefficient, target):
        rows = pl.ds(3 * group, 3)

        def step(index, carry):
            sums = [jnp.zeros((3, 8, TILE), jnp.float32) for _ in range(2)]
            for pair in range(PAIRS):
                lanes = pl.ds(pair * TILE, TILE)
                straight, turned_pair = source[rows, :, lanes], other[rows, :, lanes]
                for which in range(2):
                    sums[which] += coefficient(2 * index + which, 2 * pair) * straight
                    sums[which] += coefficient(2 * index + which, 2 * pair + 1) * turned_pair
            target[rows, :, tile_at(2 * index)] = sums[0]
            target[rows, :, tile_at(2 * index + 1)] = sums[1]
            return carry

        lax.fori_loop(0, PAIRS // 2, step, 0)

    def turn(group, source, target):
        rows = pl.ds(3 * group, 3)
        for pair in range(PAIRS):
            lanes = pl.ds(pair * TILE, TILE)
            target[rows, :, lanes] = pltpu.roll(source[rows, :, lanes], NZ, 2)

    def begin(group):
        drain(fields.at[group_rows(group)], trade_recv.at[1 + group])
        turn(group, fields, swapped)
        across_heights(
            group,
            fields,
            swapped,
            lambda pair, row: derivative[pair, pl.ds(row, 1), :],
            slopes,
        )
        send_heights(group)
        keep_heights(group)

    def shift():
        @pl.when(side == 0)
        def _():
            send(fields, later, later_send, later_recv, across)

        @pl.when(core * side == 1)
        def _():
            send(fields, later, later_send, later_recv, (seg, space - 4))

        @pl.when(core * (1 - side) == 1)
        def _():
            for group in range(3):
                send(
                    own[group],
                    later.at[group_rows(group)],
                    home_send.at[3 + group],
                    later_recv,
                    (seg - 1, space),
                )

    lane = lax.broadcasted_iota(jnp.int32, (8, TILE), 1)
    low_half = lane < NZ

    def solve_rows(pair, carry):
        even = wall_v[pl.ds(2 * pair, 8, stride=NY), :]
        odd = wall_v[pl.ds(2 * pair + 1, 8, stride=NY), :]

        def spread(value, column):
            return jnp.broadcast_to(value[:, column : column + 1], (8, TILE))

        for other in range(PAIRS):
            solve[pair, 2 * other] = jnp.where(
                low_half, spread(even, 2 * other), spread(odd, 2 * other + 1)
            )
            solve[pair, 2 * other + 1] = jnp.where(
                low_half, spread(even, 2 * other + 1), spread(odd, 2 * other)
            )
        return carry

    def kept():
        rows = mask_v[pl.ds(pl.multiple_of(place * 8, 8), 8), :].astype(jnp.float32)
        return jnp.concatenate([rows, rows], axis=1) * damping[...]

    def transform(group):
        wait_heights(group)

        def modes(unit):
            value = got[group, unit].reshape(3, NX, 3 * TILE)
            return stacked(jnp.concatenate([value[0], value[1], value[2]], axis=1), 0)

        def by_rows(value):
            return [value[:, c * TILE : (c + 1) * TILE] for c in range(9)]

        in_x = mul(x_forward[...], modes(0))
        in_x_wall = mul(x_forward[pl.ds(0, NX), :], modes(1))
        plain = jnp.concatenate(by_rows(in_x[:NX]), axis=0)
        rest = jnp.concatenate(by_rows(in_x[NX:]) + by_rows(in_x_wall), axis=0)
        pair = mul(stacked(plain, 1), z_forward[...])
        single = mul(stacked(rest, 1), z_forward[:, pl.ds(0, TILE)])
        total = [None] * 9
        for index in range(3):

            def field(value, c):
                row = (3 * c + index) * NX
                return value[row : row + NX]

            physical = [field(pair[:, :TILE], c) for c in range(3)]
            span = [field(pair[:, TILE:], c) for c in range(3)]
            stream = [field(single, c) for c in range(3)]
            slope = [field(single, c + 3) for c in range(3)]
            if group == 0:
                for c in range(3):
                    flow[index, c] = physical[c]
                    flow[index, 3 + c] = stream[c]
                    flow[index, 6 + c] = slope[c]
                    flow[index, 9 + c] = span[c]
                u, v, w = physical
            else:
                u, v, w = (flow[index, c] for c in range(3))
            u = u + heights[lax.min(first_pair + index, PAIRS - 1)]
            for c in range(3):
                value = u * stream[c] + v * slope[c] + w * span[c]
                if group > 0:
                    value += (
                        physical[0] * flow[index, 3 + c]
                        + physical[1] * flow[index, 6 + c]
                        + physical[2] * flow[index, 9 + c]
                    )
                if c == 0:
                    value += physical[1]
                total[3 * c + index] = value
        in_k = mul(stacked(jnp.concatenate(total, axis=0), 1), z_back[...])
        in_k = jnp.concatenate([in_k[c * NX : (c + 1) * NX] for c in range(9)], axis=1)
        in_m = mul(x_back[...], stacked(in_k, 0))
        for c in range(3):
            outgoing[group, c] = in_m[:, 3 * c * TILE : 3 * (c + 1) * TILE]

        def rows_of(other):
            return pl.ds(pl.multiple_of(other * 8, 8), 8)

        for way, (kind, hop) in enumerate(opposite):
            other, _ = member(kind, 2)
            _, relay = member(core, hop)
            send_tiles(
                slot(outgoing, group, everything, rows_of(other)),
                slot(passing_back, group, way, everything, everything),
                count == 3,
                back_send.at[group],
                pass_back_recv.at[group, way],
                relay,
            )
        for kind, hop in direct:
            other, device = member(kind, hop)
            send_tiles(
                slot(outgoing, group, everything, rows_of(other)),
                band_of(returned, first_pair, group, everything, everything),
                count == 3,
                back_send.at[group],
                back_recv.at[group],
                device,
            )

        mine = rows_of(place)
        returned[group, :, :, tile_at(first_pair, 2)] = outgoing[
            group, :, mine, pl.ds(0, 2 * TILE)
        ]

        @pl.when(count == 3)
        def _():
            returned[group, :, :, tile_at(first_pair + 2)] = outgoing[
                group, :, mine, pl.ds(2 * TILE, TILE)
            ]

    def pass_back(group):
        for way, (kind, hop) in enumerate(opposite):
            origin, _ = member(core, hop + 2)
            _, device = member(kind, hop)
            origin_first, origin_count = band(origin)
            held = slot(passing_back, group, way, everything, everything)
            drain_tiles(held, origin_count == 3, pass_back_recv.at[group, way])
            send_tiles(
                held,
                band_of(returned, origin_first, group, everything, everything),
                origin_count == 3,
                pass_back_send.at[group, way],
                back_recv.at[group],
                device,
            )

    def finish(group, keep):
        wait_pairs(returned.at[0], back_recv.at[group])
        rows = group_rows(group)
        for pair in range(PAIRS):
            lanes = pl.ds(pair * TILE, TILE)
            value = keep * (fields[rows, :, lanes] + returned[group, :, :, lanes])
            forced[rows, :, lanes] = value
            turned[rows, :, lanes] = pltpu.roll(value, NZ, 2)
        across_heights(
            group, forced, turned, lambda pair, row: solve[pair, row], ends
        )
        if group == 0:
            drain(later, later_recv)
        gap = ends[rows] - later[rows]
        gaps[rows] = gap

        @pl.when(traded)
        def _():
            send(
                gaps.at[rows],
                gaps_home.at[rows],
                home_send.at[group],
                home_recv.at[group],
                trader,
            )

        @pl.when(jnp.logical_not(traded))
        def _():
            gaps_home[rows] = gap

    drain(wall_v, trade_recv.at[0])
    lax.fori_loop(0, PAIRS, solve_rows, 0)
    loads[0].wait()
    begin(0)
    begin(1)
    pass_heights(0)
    begin(2)
    shift()
    pass_heights(1)
    for load in loads[1:]:
        load.wait()
    keep = kept()
    transform(0)
    pass_heights(2)
    transform(1)
    pass_back(0)
    transform(2)
    pass_back(1)
    finish(0, keep)
    pass_back(2)
    finish(1, keep)
    finish(2, keep)

    def products(index, sums):
        lanes = tile_at(index)
        start = [fields[group_rows(g), :, lanes] for g in range(3)]
        gap = [gaps[group_rows(g), :, lanes] for g in range(3)]
        drift = ends[group_rows(0), :, lanes] - start[0]
        terms = [
            drift * start[1],
            drift * start[2],
            gap[1] * gap[1],
            gap[2] * gap[2],
            gap[1] * gap[0],
            gap[2] * gap[0],
            gap[1] * gap[2],
        ]
        return tuple(s + t[0] + t[1] + t[2] for s, t in zip(sums, terms))

    sums = lax.fori_loop(
        0, PAIRS, products, tuple(jnp.zeros((8, TILE), jnp.float32) for _ in range(7))
    )
    column = lax.broadcasted_iota(jnp.int32, (1, TILE), 1)
    message = jnp.zeros((1, TILE), jnp.float32)
    for index, value in enumerate(sums):
        total = jnp.sum(jnp.sum(value, axis=0, keepdims=True), axis=1, keepdims=True)
        message = jnp.where(column == index, total, message)

    def exchange(which, slots, me, size, device, value):
        slots[me] = value
        for step in range(1, size):
            pltpu.make_async_remote_copy(
                src_ref=slots.at[me],
                dst_ref=slots.at[me],
                send_sem=sum_send.at[which],
                recv_sem=sum_recv.at[which],
                device_id=device(step),
                device_id_type=MESH,
            ).start()
        if size > 1:
            drain(slots.at[pl.ds(0, size - 1)], sum_recv.at[which])
        return jnp.sum(slots[...], axis=0)

    slots = [ring_sums, side_sums, far_sums]
    for which, me in enumerate([place, side_me, high]):
        message = exchange(which, slots[which], me, *rounds[which], message)

    def number(index):
        return message[:, index : index + 1]

    root = 1.0 / math.sqrt(nseg * 3 * NX * LANES)
    border = [number(0) * root, number(1) * root]
    diag = [number(2) + border[0] * border[0], number(3) + border[1] * border[1]]
    first = [-number(4) / diag[0], -number(5) / diag[1]]
    cross = number(6) + border[0] * border[1]
    weight = [
        first[0] - first[1] * cross / diag[0],
        first[1] - first[0] * cross / diag[1],
    ]
    weight = [jnp.broadcast_to(value, (8, TILE)) for value in weight]

    @pl.when(traded)
    def _():
        for group in range(3):
            drain(gaps_home.at[group_rows(group)], home_recv.at[group])

    def write(index, carry):
        lanes = tile_at(index)
        for source, target in ((home, corrected), (gaps_home, new_residual)):
            target[0, :, :, lanes] = (
                source[pl.ds(0, 3), :, lanes]
                + weight[0] * source[pl.ds(3, 3), :, lanes]
                + weight[1] * source[pl.ds(6, 3), :, lanes]
            )
        return carry

    lax.fori_loop(0, PAIRS, write, 0)

    for group in range(3):
        wait_pairs(pack.at[:, pl.ds(0, 3)], out_send.at[group])
    for group in range(3):
        @pl.when(count == 3)
        def _():
            drain(outgoing.at[group, :, pl.ds(0, 56), pl.ds(0, 3 * TILE)], back_send.at[group])

        @pl.when(count == 2)
        def _():
            drain(outgoing.at[group, :, pl.ds(0, 56), pl.ds(0, 2 * TILE)], back_send.at[group])

    for group in range(3):
        for way, (kind, hop) in enumerate(opposite):
            other, _ = member(kind, hop)
            _, other_count = band(other)
            origin, _ = member(core, hop + 2)
            _, origin_count = band(origin)
            drain_tiles(
                slot(passing, group, way, everything, everything, everything),
                other_count == 3,
                pass_send.at[group, way],
            )
            drain_tiles(
                slot(passing_back, group, way, everything, everything),
                origin_count == 3,
                pass_back_send.at[group, way],
            )

    @pl.when(traded)
    def _():
        for group in range(3):
            drain(fields.at[group_rows(group)], trade_send.at[1 + group])
            drain(gaps.at[group_rows(group)], home_send.at[group])
        drain(wall_v, trade_send.at[0])

    @pl.when(jnp.logical_or(side == 0, core * side == 1))
    def _():
        drain(later, later_send)

    @pl.when(core * (1 - side) == 1)
    def _():
        for group in range(3):
            drain(home.at[group_rows(group)], home_send.at[3 + group])

    for which, (size, _) in enumerate(rounds):
        if size > 1:
            drain(slots[which].at[pl.ds(0, size - 1)], sum_send.at[which])


def local(nseg, constants, states, tangent_panel, wall_inverse, keep_mask):
    operands = (
        states,
        tangent_panel,
        wall_inverse.reshape(8 * NY, NY),
        keep_mask,
        *[jnp.asarray(value) for value in constants],
    )
    f32 = jnp.float32
    sem = pltpu.SemaphoreType.DMA
    whole = (9, 8, LANES)
    scratch = [
        *[pltpu.VMEM(value.shape, value.dtype) for value in constants],
        pltpu.VMEM((8 * NY, NY), f32),
        pltpu.VMEM((NX, NZ), jnp.int32),
        pltpu.VMEM(whole, f32),
        pltpu.VMEM((2, *whole), f32),
        pltpu.VMEM(whole, f32),
        pltpu.VMEM((3, 2, 3, 8, 8, 3 * TILE), f32),
        pltpu.VMEM((3, 2, 2, 3, 8, 3 * TILE), f32),
        pltpu.VMEM((3, 12, NX, TILE), f32),
        pltpu.VMEM((3, 3, NX, 3 * TILE), f32),
        pltpu.VMEM((3, 2, 3, 8, 3 * TILE), f32),
        pltpu.VMEM((3, 3, 8, LANES), f32),
        pltpu.VMEM((PAIRS, 2 * PAIRS, 8, TILE), f32),
        *[pltpu.VMEM(whole, f32)] * 6,
        pltpu.VMEM((8, 1, TILE), f32),
        pltpu.VMEM((2 * min(4, nseg // 2), 1, TILE), f32),
        pltpu.VMEM((nseg // 2 // min(4, nseg // 2), 1, TILE), f32),
        sem((11,)),
        sem((4,)),
        sem((4,)),
        sem((3,)),
        sem((3,)),
        sem((3, 2)),
        sem((3, 2)),
        sem((3,)),
        sem((3,)),
        sem((3, 2)),
        sem((3, 2)),
        sem,
        sem,
        sem((6,)),
        sem((3,)),
        sem((3,)),
        sem((3,)),
    ]
    return pl.pallas_call(
        functools.partial(kernel, nseg),
        out_shape=[jax.ShapeDtypeStruct((1, 3, 8, LANES), f32)] * 2,
        in_specs=[pl.BlockSpec(memory_space=pl.ANY)] * len(operands),
        out_specs=[pl.BlockSpec(memory_space=pltpu.VMEM)] * 2,
        scratch_shapes=scratch,
        compiler_params=pltpu.CompilerParams(
            collective_id=0, has_side_effects=True, vmem_limit_bytes=64 * 1024 * 1024
        ),
        name="newton_step",
    )(*operands)


def solution(mesh):
    return jax.shard_map(
        functools.partial(local, mesh.shape["seg"], tables()),
        mesh=mesh,
        in_specs=(
            P("seg", None, "space", None),
            P("seg", None, None, "space", None),
            P("space", None, None),
            P(),
        ),
        out_specs=(P("seg", None, "space", None), P("seg", None, "space", None)),
        check_vma=False,
    )
```

```python
import functools
import math

import jax
import jax.numpy as jnp
import ml_dtypes
import numpy as np
from jax import lax
from jax.experimental import pallas as pl
from jax.experimental.pallas import tpu as pltpu
from jax.sharding import PartitionSpec as P

TIME_STEP = 0.005
VISCOSITY = 0.0025
STREAM_WAVE = 1.0
SPAN_WAVE = 2.0
MESH = pl.DeviceIdType.MESH
NX, NY, NZ = 64, 40, 64
TILE = 128
PAIRS = NY // 2
LANES = NY * NZ


def fourier_basis(length, stretch):
    mode = np.arange(length)[:, None]
    point = np.arange(length)[None, :]
    wave = np.where(mode == length - 1, length // 2, (mode + 1) // 2)
    phase = 2.0 * math.pi / length * (wave * point % length)
    edge = (mode == 0) | (mode == length - 1)
    amplitude = np.where(edge, math.sqrt(1.0 / length), math.sqrt(2.0 / length))
    cosine = (mode % 2 == 1) | (mode == 0)
    basis = amplitude * np.where(cosine, np.cos(phase), np.sin(phase))
    slope = stretch * wave * amplitude * np.where(cosine, -np.sin(phase), np.cos(phase))
    return basis, np.where(edge, 0.0, slope)


def wall_tables(length):
    index = np.arange(1, length + 1)
    height = np.cos(math.pi / (length + 1) * index)
    row, col = height[:, None], height[None, :]
    parity = np.where((index[:, None] + index[None, :]) % 2 == 0, 1.0, -1.0)
    same = index[:, None] == index[None, :]
    spacing = np.where(same, 1.0, row - col)
    return height, np.where(same, -row / (2.0 * (1.0 - row * row)), parity / spacing)


def span_damping(length):
    index = np.arange(length)
    wave = np.where(index == length - 1, length // 2, (index + 1) // 2)
    return 1.0 / (1.0 + TIME_STEP * VISCOSITY * (SPAN_WAVE * wave) ** 2)


def parts(matrix):
    high = matrix.astype(np.float32).astype(ml_dtypes.bfloat16)
    low = (matrix - high.astype(np.float64)).astype(np.float32).astype(ml_dtypes.bfloat16)
    return high, low


def twice(matrix):
    zero = np.zeros_like(matrix)
    return np.block([[matrix, zero], [zero, matrix]])


def tables():
    qx, sx = fourier_basis(NX, STREAM_WAVE)
    qz, sz = fourier_basis(NZ, SPAN_WAVE)
    height, wall = wall_tables(NY)
    high, low = parts(np.concatenate([qx.T, sx.T], axis=0))
    x_forward = np.concatenate([high, high, low], axis=1)
    high, low = parts(qx)
    x_back = np.concatenate([high, high, low], axis=1)
    high, low = parts(np.concatenate([twice(qz), twice(sz)], axis=1))
    z_forward = np.concatenate([high, high, low], axis=0)
    high, low = parts(-TIME_STEP * twice(qz.T))
    z_back = np.concatenate([high, high, low], axis=0)
    derivative = np.zeros((PAIRS, 2 * PAIRS, TILE))
    for half in (0, 1):
        lanes = slice(half * NZ, (half + 1) * NZ)
        derivative[:, 0::2, lanes] = wall[half::2, half::2][:, :, None]
        derivative[:, 1::2, lanes] = wall[half::2, 1 - half :: 2][:, :, None]
    heights = np.repeat(height.reshape(PAIRS, 1, 2), NZ, axis=2)
    damping = np.tile(span_damping(NZ), 2)[None, :]
    single = [value.astype(np.float32) for value in (derivative, heights, damping)]
    return (x_forward, x_back, z_forward, z_back, *single)


def band(place):
    row, side = lax.rem(place, 4), lax.div(place, 4)
    odd = lax.rem(row, 2)
    count = 3 - lax.rem(row + side, 2)
    return 5 * row + side * (3 - odd), count


def tile_at(index, tiles=1):
    return pl.ds(pl.multiple_of(index * TILE, TILE), tiles * TILE)


def split(value):
    high = value.astype(jnp.bfloat16)
    low = (value - high.astype(jnp.float32)).astype(jnp.bfloat16)
    return high, low


def stacked(value, axis):
    high, low = split(value)
    return jnp.concatenate([high, low, high], axis=axis)


def mul(a, b):
    return jnp.dot(a, b, preferred_element_type=jnp.float32)


def kernel(
    nseg,
    states,
    panel,
    wall,
    mask,
    x_forward_in,
    x_back_in,
    z_forward_in,
    z_back_in,
    derivative_in,
    heights_in,
    damping_in,
    gaps_home,
    weights,
    x_forward,
    x_back,
    z_forward,
    z_back,
    derivative,
    heights,
    damping,
    wall_v,
    mask_v,
    pack,
    swapped,
    got,
    passing,
    flow,
    outgoing,
    passing_back,
    returned,
    solve,
    forced,
    turned,
    ends,
    later,
    gaps,
    ring_sums,
    side_sums,
    far_sums,
    in_sem,
    trade_send,
    trade_recv,
    out_send,
    out_recv,
    pass_send,
    pass_recv,
    back_send,
    back_recv,
    pass_back_send,
    pass_back_recv,
    later_send,
    later_recv,
    home_send,
    home_recv,
    sum_send,
    sum_recv,
):
    seg = lax.axis_index("seg")
    space = lax.axis_index("space")
    core = lax.rem(seg, 2)
    side = lax.div(space, 4)
    row = lax.rem(space, 4)
    base = seg - core
    chip_pair = lax.div(seg, 2)
    low_count = min(4, nseg // 2)
    far_count = nseg // 2 // low_count
    side_count = 2 * low_count
    low, high = lax.rem(chip_pair, low_count), lax.div(chip_pair, low_count)
    side_me = side * low_count + low
    fields, slopes = pack.at[0], pack.at[1]
    place = core * 4 + row
    traded = core + side == 1
    trader = (base + side, place)
    first_pair, count = band(place)

    def member(kind, hop):
        where = lax.rem(row + hop + 4, 4)
        return kind * 4 + where, (base + kind, side * 4 + where)

    next_pair = lax.rem(seg + 2 * side - 2 * (1 - side) + nseg, nseg)
    across = (next_pair, space + 4 * (1 - side) - 4 * side)

    def ring_device(step):
        other = lax.rem(place + step, 8)
        return (base + lax.div(other, 4), side * 4 + lax.rem(other, 4))

    def side_device(step):
        other = lax.rem(side_me + step, side_count)
        pair = high * low_count + lax.rem(other, low_count)
        return (2 * pair + core, lax.div(other, low_count) * 4 + row)

    def far_device(step):
        return (2 * (lax.rem(high + step, far_count) * low_count + low) + core, space)

    rounds = [(8, ring_device), (side_count, side_device), (far_count, far_device)]
    barrier = pltpu.get_barrier_semaphore()

    def greet(device):
        pl.semaphore_signal(barrier, inc=1, device_id=device, device_id_type=MESH)

    @pl.when(traded)
    def _():
        greet(trader)

    for size, device in reversed(rounds):
        for step in range(1, size):
            greet(device(step))
    greet(across)

    own = [states.at[0], panel.at[0, 0], panel.at[0, 1]]

    def group_rows(group):
        return pl.ds(3 * group, 3)

    loads = [
        (derivative_in, derivative),
        (mask, mask_v),
        (x_forward_in, x_forward),
        (z_forward_in, z_forward),
        (x_back_in, x_back),
        (z_back_in, z_back),
        (heights_in, heights),
        (damping_in, damping),
    ]
    loads = [
        pltpu.make_async_copy(src, dst, in_sem.at[index])
        for index, (src, dst) in enumerate(loads)
    ]
    begins = [(own[group], fields.at[group_rows(group)]) for group in range(3)] + [(wall, wall_v)]

    @pl.when(jnp.logical_not(traded))
    def _():
        for index, (src, dst) in enumerate(begins):
            pltpu.make_async_copy(src, dst, trade_recv.at[index]).start()

    for load in loads:
        load.start()
    greetings = sum(size - 1 for size, _ in rounds) + 1

    @pl.when(traded)
    def _():
        pl.semaphore_wait(barrier, greetings + 1)

    @pl.when(jnp.logical_not(traded))
    def _():
        pl.semaphore_wait(barrier, greetings)


    def send(src, dst, send_sem, recv_sem, device):
        pltpu.make_async_remote_copy(
            src_ref=src,
            dst_ref=dst,
            send_sem=send_sem,
            recv_sem=recv_sem,
            device_id=device,
            device_id_type=MESH,
        ).start()

    def send_tiles(src, dst, three, send_sem, recv_sem, device):
        @pl.when(three)
        def _():
            send(src(3), dst(3), send_sem, recv_sem, device)

        @pl.when(jnp.logical_not(three))
        def _():
            send(src(2), dst(2), send_sem, recv_sem, device)

    @pl.when(traded)
    def _():
        for index, (src, dst) in enumerate(begins):
            send(src, dst, trade_send.at[index], trade_recv.at[index], trader)

    def slot(ref, *index):
        return lambda tiles: ref.at[(*index, pl.ds(0, tiles * TILE))]

    def band_of(ref, first, *index):
        return lambda tiles: ref.at[(*index, tile_at(first, tiles))]

    everything = slice(None)
    direct = [(1 - core, 0), (0, 1), (1, 1), (0, 3), (1, 3)]
    opposite = [(0, 1), (1, 3)]

    def send_heights(group):
        source = (pack, everything, group_rows(group), everything)
        for way, (kind, hop) in enumerate(opposite):
            other, _ = member(kind, 2)
            _, relay = member(core, hop)
            other_first, other_count = band(other)
            send_tiles(
                band_of(source[0], other_first, *source[1:]),
                slot(passing, group, way, everything, everything, everything),
                other_count == 3,
                out_send.at[group],
                pass_recv.at[group, way],
                relay,
            )
        for kind, hop in direct:
            other, device = member(kind, hop)
            other_first, other_count = band(other)
            send_tiles(
                band_of(source[0], other_first, *source[1:]),
                slot(got, group, everything, everything, place, everything),
                other_count == 3,
                out_send.at[group],
                out_recv.at[group],
                device,
            )

    def drain_tiles(ref, three, sem):
        @pl.when(three)
        def _():
            drain(ref(3), sem)

        @pl.when(jnp.logical_not(three))
        def _():
            drain(ref(2), sem)

    def pass_heights(group):
        for way, (kind, hop) in enumerate(opposite):
            origin, _ = member(core, hop + 2)
            other, device = member(kind, hop)
            _, other_count = band(other)
            held = slot(passing, group, way, everything, everything, everything)
            drain_tiles(held, other_count == 3, pass_recv.at[group, way])
            send_tiles(
                held,
                slot(got, group, everything, everything, origin, everything),
                other_count == 3,
                pass_send.at[group, way],
                out_recv.at[group],
                device,
            )

    def keep_heights(group):
        for unit in range(2):
            got[group, unit, :, place, :, pl.ds(0, 2 * TILE)] = pack[
                unit, group_rows(group), :, tile_at(first_pair, 2)
            ]

            @pl.when(count == 3)
            def _():
                got[group, unit, :, place, :, pl.ds(2 * TILE, TILE)] = pack[
                    unit, group_rows(group), :, tile_at(first_pair + 2)
                ]

    def drain(ref, sem):
        pltpu.make_async_copy(ref, ref, sem).wait()

    def wait_heights(group):
        arrived = slot(got, group, everything, everything, pl.ds(0, 7), everything)
        drain_tiles(arrived, count == 3, out_recv.at[group])

    def wait_pairs(ref, sem):
        @pl.when(count == 3)
        def _():
            drain(ref.at[..., pl.ds(0, (PAIRS - 3) * TILE)], sem)

        @pl.when(count == 2)
        def _():
            drain(ref.at[..., pl.ds(0, (PAIRS - 2) * TILE)], sem)

    def across_heights(group, source, other, coefficient, target):
        rows = pl.ds(3 * group, 3)

        def step(index, carry):
            sums = [jnp.zeros((3, 8, TILE), jnp.float32) for _ in range(2)]
            for pair in range(PAIRS):
                lanes = pl.ds(pair * TILE, TILE)
                straight, turned_pair = source[rows, :, lanes], other[rows, :, lanes]
                for which in range(2):
                    sums[which] += coefficient(2 * index + which, 2 * pair) * straight
                    sums[which] += coefficient(2 * index + which, 2 * pair + 1) * turned_pair
            target[rows, :, tile_at(2 * index)] = sums[0]
            target[rows, :, tile_at(2 * index + 1)] = sums[1]
            return carry

        lax.fori_loop(0, PAIRS // 2, step, 0)

    def turn(group, source, target):
        rows = pl.ds(3 * group, 3)
        for pair in range(PAIRS):
            lanes = pl.ds(pair * TILE, TILE)
            target[rows, :, lanes] = pltpu.roll(source[rows, :, lanes], NZ, 2)

    def begin(group):
        drain(fields.at[group_rows(group)], trade_recv.at[group])
        turn(group, fields, swapped)
        across_heights(
            group,
            fields,
            swapped,
            lambda pair, row: derivative[pair, pl.ds(row, 1), :],
            slopes,
        )
        send_heights(group)
        keep_heights(group)

    def shift():
        @pl.when(side == 0)
        def _():
            send(fields, later, later_send, later_recv, across)

        @pl.when(core * side == 1)
        def _():
            send(fields, later, later_send, later_recv, (seg, space - 4))

        @pl.when(core * (1 - side) == 1)
        def _():
            for group in range(3):
                send(
                    own[group],
                    later.at[group_rows(group)],
                    home_send.at[3 + group],
                    later_recv,
                    (seg - 1, space),
                )

    lane = lax.broadcasted_iota(jnp.int32, (8, TILE), 1)
    low_half = lane < NZ

    def solve_rows(pair, carry):
        even = wall_v[pl.ds(2 * pair, 8, stride=NY), :]
        odd = wall_v[pl.ds(2 * pair + 1, 8, stride=NY), :]

        def spread(value, column):
            return jnp.broadcast_to(value[:, column : column + 1], (8, TILE))

        for other in range(PAIRS):
            solve[pair, 2 * other] = jnp.where(
                low_half, spread(even, 2 * other), spread(odd, 2 * other + 1)
            )
            solve[pair, 2 * other + 1] = jnp.where(
                low_half, spread(even, 2 * other + 1), spread(odd, 2 * other)
            )
        return carry

    def kept():
        rows = mask_v[pl.ds(pl.multiple_of(place * 8, 8), 8), :].astype(jnp.float32)
        return jnp.concatenate([rows, rows], axis=1) * damping[...]

    def transform(group):
        wait_heights(group)

        def modes(unit):
            value = got[group, unit].reshape(3, NX, 3 * TILE)
            return stacked(jnp.concatenate([value[0], value[1], value[2]], axis=1), 0)

        def by_rows(value):
            return [value[:, c * TILE : (c + 1) * TILE] for c in range(9)]

        in_x = mul(x_forward[...], modes(0))
        in_x_wall = mul(x_forward[pl.ds(0, NX), :], modes(1))
        plain = jnp.concatenate(by_rows(in_x[:NX]), axis=0)
        rest = jnp.concatenate(by_rows(in_x[NX:]) + by_rows(in_x_wall), axis=0)
        pair = mul(stacked(plain, 1), z_forward[...])
        single = mul(stacked(rest, 1), z_forward[:, pl.ds(0, TILE)])
        total = [None] * 9
        for index in range(3):

            def field(value, c):
                row = (3 * c + index) * NX
                return value[row : row + NX]

            physical = [field(pair[:, :TILE], c) for c in range(3)]
            span = [field(pair[:, TILE:], c) for c in range(3)]
            stream = [field(single, c) for c in range(3)]
            slope = [field(single, c + 3) for c in range(3)]
            if group == 0:
                for c in range(3):
                    flow[index, c] = physical[c]
                    flow[index, 3 + c] = stream[c]
                    flow[index, 6 + c] = slope[c]
                    flow[index, 9 + c] = span[c]
                u, v, w = physical
            else:
                u, v, w = (flow[index, c] for c in range(3))
            u = u + heights[lax.min(first_pair + index, PAIRS - 1)]
            for c in range(3):
                value = u * stream[c] + v * slope[c] + w * span[c]
                if group > 0:
                    value += (
                        physical[0] * flow[index, 3 + c]
                        + physical[1] * flow[index, 6 + c]
                        + physical[2] * flow[index, 9 + c]
                    )
                if c == 0:
                    value += physical[1]
                total[3 * c + index] = value
        in_k = mul(stacked(jnp.concatenate(total, axis=0), 1), z_back[...])
        in_k = jnp.concatenate([in_k[c * NX : (c + 1) * NX] for c in range(9)], axis=1)
        in_m = mul(x_back[...], stacked(in_k, 0))
        for c in range(3):
            outgoing[group, c] = in_m[:, 3 * c * TILE : 3 * (c + 1) * TILE]

        def rows_of(other):
            return pl.ds(pl.multiple_of(other * 8, 8), 8)

        for way, (kind, hop) in enumerate(opposite):
            other, _ = member(kind, 2)
            _, relay = member(core, hop)
            send_tiles(
                slot(outgoing, group, everything, rows_of(other)),
                slot(passing_back, group, way, everything, everything),
                count == 3,
                back_send.at[group],
                pass_back_recv.at[group, way],
                relay,
            )
        for kind, hop in direct:
            other, device = member(kind, hop)
            send_tiles(
                slot(outgoing, group, everything, rows_of(other)),
                band_of(returned, first_pair, group, everything, everything),
                count == 3,
                back_send.at[group],
                back_recv.at[group],
                device,
            )

        mine = rows_of(place)
        returned[group, :, :, tile_at(first_pair, 2)] = outgoing[
            group, :, mine, pl.ds(0, 2 * TILE)
        ]

        @pl.when(count == 3)
        def _():
            returned[group, :, :, tile_at(first_pair + 2)] = outgoing[
                group, :, mine, pl.ds(2 * TILE, TILE)
            ]

    def pass_back(group):
        for way, (kind, hop) in enumerate(opposite):
            origin, _ = member(core, hop + 2)
            _, device = member(kind, hop)
            origin_first, origin_count = band(origin)
            held = slot(passing_back, group, way, everything, everything)
            drain_tiles(held, origin_count == 3, pass_back_recv.at[group, way])
            send_tiles(
                held,
                band_of(returned, origin_first, group, everything, everything),
                origin_count == 3,
                pass_back_send.at[group, way],
                back_recv.at[group],
                device,
            )

    def finish(group, keep):
        wait_pairs(returned.at[0], back_recv.at[group])
        rows = group_rows(group)
        for pair in range(PAIRS):
            lanes = pl.ds(pair * TILE, TILE)
            value = keep * (fields[rows, :, lanes] + returned[group, :, :, lanes])
            forced[rows, :, lanes] = value
            turned[rows, :, lanes] = pltpu.roll(value, NZ, 2)
        across_heights(
            group, forced, turned, lambda pair, row: solve[pair, row], ends
        )
        if group == 0:
            drain(later, later_recv)
        gap = ends[rows] - later[rows]
        gaps[rows] = gap

        @pl.when(traded)
        def _():
            send(
                gaps.at[rows],
                gaps_home.at[rows],
                home_send.at[group],
                home_recv.at[group],
                trader,
            )

        @pl.when(jnp.logical_not(traded))
        def _():
            pltpu.make_async_copy(
                gaps.at[rows], gaps_home.at[rows], home_recv.at[group]
            ).start()

    loads[0].wait()
    begin(0)
    begin(1)
    pass_heights(0)
    begin(2)
    shift()
    drain(wall_v, trade_recv.at[3])
    lax.fori_loop(0, PAIRS, solve_rows, 0)
    pass_heights(1)
    for load in loads[1:]:
        load.wait()
    keep = kept()
    transform(0)
    pass_heights(2)
    transform(1)
    pass_back(0)
    transform(2)
    pass_back(1)
    finish(0, keep)
    pass_back(2)
    finish(1, keep)
    finish(2, keep)

    def products(index, sums):
        lanes = tile_at(index)
        start = [fields[group_rows(g), :, lanes] for g in range(3)]
        gap = [gaps[group_rows(g), :, lanes] for g in range(3)]
        drift = ends[group_rows(0), :, lanes] - start[0]
        terms = [
            drift * start[1],
            drift * start[2],
            gap[1] * gap[1],
            gap[2] * gap[2],
            gap[1] * gap[0],
            gap[2] * gap[0],
            gap[1] * gap[2],
        ]
        return tuple(s + t[0] + t[1] + t[2] for s, t in zip(sums, terms))

    sums = lax.fori_loop(
        0, PAIRS, products, tuple(jnp.zeros((8, TILE), jnp.float32) for _ in range(7))
    )
    column = lax.broadcasted_iota(jnp.int32, (1, TILE), 1)
    message = jnp.zeros((1, TILE), jnp.float32)
    for index, value in enumerate(sums):
        total = jnp.sum(jnp.sum(value, axis=0, keepdims=True), axis=1, keepdims=True)
        message = jnp.where(column == index, total, message)

    def exchange(which, slots, me, size, device, value):
        slots[me] = value
        for step in range(1, size):
            pltpu.make_async_remote_copy(
                src_ref=slots.at[me],
                dst_ref=slots.at[me],
                send_sem=sum_send.at[which],
                recv_sem=sum_recv.at[which],
                device_id=device(step),
                device_id_type=MESH,
            ).start()
        if size > 1:
            drain(slots.at[pl.ds(0, size - 1)], sum_recv.at[which])
        return jnp.sum(slots[...], axis=0)

    slots = [ring_sums, side_sums, far_sums]
    for which, me in enumerate([place, side_me, high]):
        message = exchange(which, slots[which], me, *rounds[which], message)

    def number(index):
        return message[:, index : index + 1]

    root = 1.0 / math.sqrt(nseg * 3 * NX * LANES)
    border = [number(0) * root, number(1) * root]
    diag = [number(2) + border[0] * border[0], number(3) + border[1] * border[1]]
    first = [-number(4) / diag[0], -number(5) / diag[1]]
    cross = number(6) + border[0] * border[1]
    weights[pl.ds(0, 1), :] = jnp.broadcast_to(first[0] - first[1] * cross / diag[0], (1, TILE))
    weights[pl.ds(1, 1), :] = jnp.broadcast_to(first[1] - first[0] * cross / diag[1], (1, TILE))

    for group in range(3):
        drain(gaps_home.at[group_rows(group)], home_recv.at[group])
    for group in range(3):
        wait_pairs(pack.at[:, pl.ds(0, 3)], out_send.at[group])
    for group in range(3):
        @pl.when(count == 3)
        def _():
            drain(outgoing.at[group, :, pl.ds(0, 56), pl.ds(0, 3 * TILE)], back_send.at[group])

        @pl.when(count == 2)
        def _():
            drain(outgoing.at[group, :, pl.ds(0, 56), pl.ds(0, 2 * TILE)], back_send.at[group])

    for group in range(3):
        for way, (kind, hop) in enumerate(opposite):
            other, _ = member(kind, hop)
            _, other_count = band(other)
            origin, _ = member(core, hop + 2)
            _, origin_count = band(origin)
            drain_tiles(
                slot(passing, group, way, everything, everything, everything),
                other_count == 3,
                pass_send.at[group, way],
            )
            drain_tiles(
                slot(passing_back, group, way, everything, everything),
                origin_count == 3,
                pass_back_send.at[group, way],
            )

    @pl.when(traded)
    def _():
        for group in range(3):
            drain(fields.at[group_rows(group)], trade_send.at[group])
            drain(gaps.at[group_rows(group)], home_send.at[group])
        drain(wall_v, trade_send.at[3])

    @pl.when(jnp.logical_or(side == 0, core * side == 1))
    def _():
        drain(later, later_send)

    @pl.when(core * (1 - side) == 1)
    def _():
        for group in range(3):
            drain(fields.at[group_rows(group)], home_send.at[3 + group])

    for which, (size, _) in enumerate(rounds):
        if size > 1:
            drain(slots[which].at[pl.ds(0, size - 1)], sum_send.at[which])


def final_kernel(states, panel, gaps, weights, corrected, new_residual):
    a = jnp.broadcast_to(weights[pl.ds(0, 1), :], (8, TILE))
    b = jnp.broadcast_to(weights[pl.ds(1, 1), :], (8, TILE))
    for pair in range(PAIRS):
        lanes = pl.ds(pair * TILE, TILE)
        corrected[0, :, :, lanes] = (
            states[0, :, :, lanes] + a * panel[0, 0, :, :, lanes] + b * panel[0, 1, :, :, lanes]
        )
        new_residual[0, :, :, lanes] = (
            gaps[pl.ds(0, 3), :, lanes]
            + a * gaps[pl.ds(3, 3), :, lanes]
            + b * gaps[pl.ds(6, 3), :, lanes]
        )


def local(nseg, constants, states, tangent_panel, wall_inverse, keep_mask):
    operands = (
        states,
        tangent_panel,
        wall_inverse.reshape(8 * NY, NY),
        keep_mask,
        *[jnp.asarray(value) for value in constants],
    )
    f32 = jnp.float32
    sem = pltpu.SemaphoreType.DMA
    whole = (9, 8, LANES)
    scratch = [
        *[pltpu.VMEM(value.shape, value.dtype) for value in constants],
        pltpu.VMEM((8 * NY, NY), f32),
        pltpu.VMEM((NX, NZ), jnp.int32),
        pltpu.VMEM((2, *whole), f32),
        pltpu.VMEM(whole, f32),
        pltpu.VMEM((3, 2, 3, 8, 8, 3 * TILE), f32),
        pltpu.VMEM((3, 2, 2, 3, 8, 3 * TILE), f32),
        pltpu.VMEM((3, 12, NX, TILE), f32),
        pltpu.VMEM((3, 3, NX, 3 * TILE), f32),
        pltpu.VMEM((3, 2, 3, 8, 3 * TILE), f32),
        pltpu.VMEM((3, 3, 8, LANES), f32),
        pltpu.VMEM((PAIRS, 2 * PAIRS, 8, TILE), f32),
        *[pltpu.VMEM(whole, f32)] * 5,
        pltpu.VMEM((8, 1, TILE), f32),
        pltpu.VMEM((2 * min(4, nseg // 2), 1, TILE), f32),
        pltpu.VMEM((nseg // 2 // min(4, nseg // 2), 1, TILE), f32),
        sem((8,)),
        sem((4,)),
        sem((4,)),
        sem((3,)),
        sem((3,)),
        sem((3, 2)),
        sem((3, 2)),
        sem((3,)),
        sem((3,)),
        sem((3, 2)),
        sem((3, 2)),
        sem,
        sem,
        sem((6,)),
        sem((3,)),
        sem((3,)),
        sem((3,)),
    ]
    vmem, hbm = pl.BlockSpec(memory_space=pltpu.VMEM), pl.BlockSpec(memory_space=pl.ANY)
    grant = 64 * 1024 * 1024
    gaps, weights = pl.pallas_call(
        functools.partial(kernel, nseg),
        out_shape=[
            jax.ShapeDtypeStruct(whole, f32),
            jax.ShapeDtypeStruct((2, TILE), f32),
        ],
        in_specs=[hbm] * len(operands),
        out_specs=[hbm, vmem],
        scratch_shapes=scratch,
        compiler_params=pltpu.CompilerParams(
            collective_id=0, has_side_effects=True, vmem_limit_bytes=grant
        ),
        name="newton_step",
    )(*operands)
    result = jax.ShapeDtypeStruct((1, 3, 8, LANES), f32)
    return pl.pallas_call(
        final_kernel,
        out_shape=[result, result],
        in_specs=[vmem] * 4,
        out_specs=[vmem, vmem],
        compiler_params=pltpu.CompilerParams(vmem_limit_bytes=grant),
        name="newton_final",
    )(states, tangent_panel, gaps, weights)


def solution(mesh):
    return jax.shard_map(
        functools.partial(local, mesh.shape["seg"], tables()),
        mesh=mesh,
        in_specs=(
            P("seg", None, "space", None),
            P("seg", None, None, "space", None),
            P("space", None, None),
            P(),
        ),
        out_specs=(P("seg", None, "space", None), P("seg", None, "space", None)),
        check_vma=False,
    )
```

```python
import functools
import math

import jax
import jax.numpy as jnp
import ml_dtypes
import numpy as np
from jax import lax
from jax.experimental import pallas as pl
from jax.experimental.pallas import tpu as pltpu
from jax.sharding import PartitionSpec as P

TIME_STEP = 0.005
VISCOSITY = 0.0025
STREAM_WAVE = 1.0
SPAN_WAVE = 2.0
MESH = pl.DeviceIdType.MESH
NX, NY, NZ = 64, 40, 64
TILE = 128
PAIRS = NY // 2
LANES = NY * NZ


def fourier_basis(length, stretch):
    mode = np.arange(length)[:, None]
    point = np.arange(length)[None, :]
    wave = np.where(mode == length - 1, length // 2, (mode + 1) // 2)
    phase = 2.0 * math.pi / length * (wave * point % length)
    edge = (mode == 0) | (mode == length - 1)
    amplitude = np.where(edge, math.sqrt(1.0 / length), math.sqrt(2.0 / length))
    cosine = (mode % 2 == 1) | (mode == 0)
    basis = amplitude * np.where(cosine, np.cos(phase), np.sin(phase))
    slope = stretch * wave * amplitude * np.where(cosine, -np.sin(phase), np.cos(phase))
    return basis, np.where(edge, 0.0, slope)


def wall_tables(length):
    index = np.arange(1, length + 1)
    height = np.cos(math.pi / (length + 1) * index)
    row, col = height[:, None], height[None, :]
    parity = np.where((index[:, None] + index[None, :]) % 2 == 0, 1.0, -1.0)
    same = index[:, None] == index[None, :]
    spacing = np.where(same, 1.0, row - col)
    return height, np.where(same, -row / (2.0 * (1.0 - row * row)), parity / spacing)


def span_damping(length):
    index = np.arange(length)
    wave = np.where(index == length - 1, length // 2, (index + 1) // 2)
    return 1.0 / (1.0 + TIME_STEP * VISCOSITY * (SPAN_WAVE * wave) ** 2)


def parts(matrix):
    high = matrix.astype(np.float32).astype(ml_dtypes.bfloat16)
    low = (matrix - high.astype(np.float64)).astype(np.float32).astype(ml_dtypes.bfloat16)
    return high, low


def twice(matrix):
    zero = np.zeros_like(matrix)
    return np.block([[matrix, zero], [zero, matrix]])


def tables():
    qx, sx = fourier_basis(NX, STREAM_WAVE)
    qz, sz = fourier_basis(NZ, SPAN_WAVE)
    height, wall = wall_tables(NY)
    high, low = parts(np.concatenate([qx.T, sx.T], axis=0))
    x_forward = np.concatenate([high, high, low], axis=1)
    high, low = parts(qx)
    x_back = np.concatenate([high, high, low], axis=1)
    high, low = parts(np.concatenate([twice(qz), twice(sz)], axis=1))
    z_forward = np.concatenate([high, high, low], axis=0)
    high, low = parts(-TIME_STEP * twice(qz.T))
    z_back = np.concatenate([high, high, low], axis=0)
    derivative = np.zeros((PAIRS, 2 * PAIRS, TILE))
    for half in (0, 1):
        lanes = slice(half * NZ, (half + 1) * NZ)
        derivative[:, 0::2, lanes] = wall[half::2, half::2][:, :, None]
        derivative[:, 1::2, lanes] = wall[half::2, 1 - half :: 2][:, :, None]
    heights = np.repeat(height.reshape(PAIRS, 1, 2), NZ, axis=2)
    damping = np.tile(span_damping(NZ), 2)[None, :]
    single = [value.astype(np.float32) for value in (derivative, heights, damping)]
    return (x_forward, x_back, z_forward, z_back, *single)


def band(place):
    row, side = lax.rem(place, 4), lax.div(place, 4)
    odd = lax.rem(row, 2)
    count = 3 - lax.rem(row + side, 2)
    return 5 * row + side * (3 - odd), count


def tile_at(index, tiles=1):
    return pl.ds(pl.multiple_of(index * TILE, TILE), tiles * TILE)


def split(value):
    high = value.astype(jnp.bfloat16)
    low = (value - high.astype(jnp.float32)).astype(jnp.bfloat16)
    return high, low


def stacked(value, axis):
    high, low = split(value)
    return jnp.concatenate([high, low, high], axis=axis)


def mul(a, b):
    return jnp.dot(a, b, preferred_element_type=jnp.float32)


def kernel(
    nseg,
    states,
    panel,
    wall,
    mask,
    x_forward_in,
    x_back_in,
    z_forward_in,
    z_back_in,
    derivative_in,
    heights_in,
    damping_in,
    corrected,
    new_residual,
    x_forward,
    x_back,
    z_forward,
    z_back,
    derivative,
    heights,
    damping,
    wall_v,
    mask_v,
    home,
    pack,
    swapped,
    got,
    flow,
    outgoing,
    returned,
    solve,
    forced,
    turned,
    ends,
    later,
    gaps,
    gaps_home,
    ring_sums,
    side_sums,
    far_sums,
    in_sem,
    trade_send,
    trade_recv,
    out_send,
    out_recv,
    back_send,
    back_recv,
    later_send,
    later_recv,
    home_send,
    home_recv,
    sum_send,
    sum_recv,
):
    seg = lax.axis_index("seg")
    space = lax.axis_index("space")
    core = lax.rem(seg, 2)
    side = lax.div(space, 4)
    row = lax.rem(space, 4)
    base = seg - core
    chip_pair = lax.div(seg, 2)
    low_count = min(4, nseg // 2)
    far_count = nseg // 2 // low_count
    side_count = 2 * low_count
    low, high = lax.rem(chip_pair, low_count), lax.div(chip_pair, low_count)
    side_me = side * low_count + low
    fields, slopes = pack.at[0], pack.at[1]
    place = core * 4 + row
    traded = core + side == 1
    trader = (base + side, place)
    first_pair, count = band(place)

    def member(kind, hop):
        where = lax.rem(row + hop + 4, 4)
        return kind * 4 + where, (base + kind, side * 4 + where)

    next_pair = lax.rem(seg + 2 * side - 2 * (1 - side) + nseg, nseg)
    across = (next_pair, space + 4 * (1 - side) - 4 * side)

    def ring_device(step):
        other = lax.rem(place + step, 8)
        return (base + lax.div(other, 4), side * 4 + lax.rem(other, 4))

    def side_device(step):
        other = lax.rem(side_me + step, side_count)
        pair = high * low_count + lax.rem(other, low_count)
        return (2 * pair + core, lax.div(other, low_count) * 4 + row)

    def far_device(step):
        return (2 * (lax.rem(high + step, far_count) * low_count + low) + core, space)

    rounds = [(8, ring_device), (side_count, side_device), (far_count, far_device)]
    barrier = pltpu.get_barrier_semaphore()

    def greet(device):
        pl.semaphore_signal(barrier, inc=1, device_id=device, device_id_type=MESH)

    @pl.when(traded)
    def _():
        greet(trader)

    for size, device in rounds:
        for step in range(1, size):
            greet(device(step))
    greet(across)

    own = [states.at[0], panel.at[0, 0], panel.at[0, 1]]

    def group_rows(group):
        return pl.ds(3 * group, 3)

    loads = [
        (derivative_in, derivative),
        (mask, mask_v),
        (x_forward_in, x_forward),
        (z_forward_in, z_forward),
        (x_back_in, x_back),
        (z_back_in, z_back),
        (heights_in, heights),
        (damping_in, damping),
        *[(own[group], home.at[group_rows(group)]) for group in range(3)],
    ]
    loads = [
        pltpu.make_async_copy(src, dst, in_sem.at[index])
        for index, (src, dst) in enumerate(loads)
    ]
    begins = [(wall, wall_v)] + [(own[group], fields.at[group_rows(group)]) for group in range(3)]

    @pl.when(jnp.logical_not(traded))
    def _():
        for index, (src, dst) in enumerate(begins):
            pltpu.make_async_copy(src, dst, trade_recv.at[index]).start()

    for load in loads:
        load.start()
    greetings = sum(size - 1 for size, _ in rounds) + 1

    @pl.when(traded)
    def _():
        pl.semaphore_wait(barrier, greetings + 1)

    @pl.when(jnp.logical_not(traded))
    def _():
        pl.semaphore_wait(barrier, greetings)


    def send(src, dst, send_sem, recv_sem, device):
        pltpu.make_async_remote_copy(
            src_ref=src,
            dst_ref=dst,
            send_sem=send_sem,
            recv_sem=recv_sem,
            device_id=device,
            device_id_type=MESH,
        ).start()

    def send_tiles(src, dst, three, send_sem, recv_sem, device):
        @pl.when(three)
        def _():
            send(src(3), dst(3), send_sem, recv_sem, device)

        @pl.when(jnp.logical_not(three))
        def _():
            send(src(2), dst(2), send_sem, recv_sem, device)

    @pl.when(traded)
    def _():
        for index, (src, dst) in enumerate(begins):
            send(src, dst, trade_send.at[index], trade_recv.at[index], trader)

    def slot(ref, *index):
        return lambda tiles: ref.at[(*index, pl.ds(0, tiles * TILE))]

    def band_of(ref, first, *index):
        return lambda tiles: ref.at[(*index, tile_at(first, tiles))]

    everything = slice(None)
    direct = [(0, 2), (1, 2), (0, 1), (1, 1), (0, 3), (1, 3), (1 - core, 0)]

    def send_heights(group):
        source = (pack, everything, group_rows(group), everything)
        for kind, hop in direct:
            other, device = member(kind, hop)
            other_first, other_count = band(other)
            send_tiles(
                band_of(source[0], other_first, *source[1:]),
                slot(got, group, everything, everything, place, everything),
                other_count == 3,
                out_send.at[group],
                out_recv.at[group],
                device,
            )

    def drain_tiles(ref, three, sem):
        @pl.when(three)
        def _():
            drain(ref(3), sem)

        @pl.when(jnp.logical_not(three))
        def _():
            drain(ref(2), sem)

    def keep_heights(group):
        for unit in range(2):
            got[group, unit, :, place, :, pl.ds(0, 2 * TILE)] = pack[
                unit, group_rows(group), :, tile_at(first_pair, 2)
            ]

            @pl.when(count == 3)
            def _():
                got[group, unit, :, place, :, pl.ds(2 * TILE, TILE)] = pack[
                    unit, group_rows(group), :, tile_at(first_pair + 2)
                ]

    def drain(ref, sem):
        pltpu.make_async_copy(ref, ref, sem).wait()

    def wait_heights(group):
        arrived = slot(got, group, everything, everything, pl.ds(0, 7), everything)
        drain_tiles(arrived, count == 3, out_recv.at[group])

    def wait_pairs(ref, sem):
        @pl.when(count == 3)
        def _():
            drain(ref.at[..., pl.ds(0, (PAIRS - 3) * TILE)], sem)

        @pl.when(count == 2)
        def _():
            drain(ref.at[..., pl.ds(0, (PAIRS - 2) * TILE)], sem)

    def across_heights(group, source, other, coefficient, target):
        rows = pl.ds(3 * group, 3)

        def step(index, carry):
            sums = [jnp.zeros((3, 8, TILE), jnp.float32) for _ in range(2)]
            for pair in range(PAIRS):
                lanes = pl.ds(pair * TILE, TILE)
                straight, turned_pair = source[rows, :, lanes], other[rows, :, lanes]
                for which in range(2):
                    sums[which] += coefficient(2 * index + which, 2 * pair) * straight
                    sums[which] += coefficient(2 * index + which, 2 * pair + 1) * turned_pair
            target[rows, :, tile_at(2 * index)] = sums[0]
            target[rows, :, tile_at(2 * index + 1)] = sums[1]
            return carry

        lax.fori_loop(0, PAIRS // 2, step, 0)

    def turn(group, source, target):
        rows = pl.ds(3 * group, 3)
        for pair in range(PAIRS):
            lanes = pl.ds(pair * TILE, TILE)
            target[rows, :, lanes] = pltpu.roll(source[rows, :, lanes], NZ, 2)

    def begin(group):
        drain(fields.at[group_rows(group)], trade_recv.at[1 + group])
        turn(group, fields, swapped)
        across_heights(
            group,
            fields,
            swapped,
            lambda pair, row: derivative[pair, pl.ds(row, 1), :],
            slopes,
        )
        send_heights(group)
        keep_heights(group)

    def shift():
        @pl.when(side == 0)
        def _():
            send(fields, later, later_send, later_recv, across)

        @pl.when(core * side == 1)
        def _():
            send(fields, later, later_send, later_recv, (seg, space - 4))

        @pl.when(core * (1 - side) == 1)
        def _():
            for group in range(3):
                send(
                    own[group],
                    later.at[group_rows(group)],
                    home_send.at[3 + group],
                    later_recv,
                    (seg - 1, space),
                )

    lane = lax.broadcasted_iota(jnp.int32, (8, TILE), 1)
    low_half = lane < NZ

    def solve_rows(pair, carry):
        even = wall_v[pl.ds(2 * pair, 8, stride=NY), :]
        odd = wall_v[pl.ds(2 * pair + 1, 8, stride=NY), :]

        def spread(value, column):
            return jnp.broadcast_to(value[:, column : column + 1], (8, TILE))

        for other in range(PAIRS):
            solve[pair, 2 * other] = jnp.where(
                low_half, spread(even, 2 * other), spread(odd, 2 * other + 1)
            )
            solve[pair, 2 * other + 1] = jnp.where(
                low_half, spread(even, 2 * other + 1), spread(odd, 2 * other)
            )
        return carry

    def kept():
        rows = mask_v[pl.ds(pl.multiple_of(place * 8, 8), 8), :].astype(jnp.float32)
        return jnp.concatenate([rows, rows], axis=1) * damping[...]

    def transform(group):
        wait_heights(group)

        def modes(unit):
            value = got[group, unit].reshape(3, NX, 3 * TILE)
            return stacked(jnp.concatenate([value[0], value[1], value[2]], axis=1), 0)

        def by_rows(value):
            return [value[:, c * TILE : (c + 1) * TILE] for c in range(9)]

        in_x = mul(x_forward[...], modes(0))
        in_x_wall = mul(x_forward[pl.ds(0, NX), :], modes(1))
        plain = jnp.concatenate(by_rows(in_x[:NX]), axis=0)
        rest = jnp.concatenate(by_rows(in_x[NX:]) + by_rows(in_x_wall), axis=0)
        pair = mul(stacked(plain, 1), z_forward[...])
        single = mul(stacked(rest, 1), z_forward[:, pl.ds(0, TILE)])
        total = [None] * 9
        for index in range(3):

            def field(value, c):
                row = (3 * c + index) * NX
                return value[row : row + NX]

            physical = [field(pair[:, :TILE], c) for c in range(3)]
            span = [field(pair[:, TILE:], c) for c in range(3)]
            stream = [field(single, c) for c in range(3)]
            slope = [field(single, c + 3) for c in range(3)]
            if group == 0:
                for c in range(3):
                    flow[index, c] = physical[c]
                    flow[index, 3 + c] = stream[c]
                    flow[index, 6 + c] = slope[c]
                    flow[index, 9 + c] = span[c]
                u, v, w = physical
            else:
                u, v, w = (flow[index, c] for c in range(3))
            u = u + heights[lax.min(first_pair + index, PAIRS - 1)]
            for c in range(3):
                value = u * stream[c] + v * slope[c] + w * span[c]
                if group > 0:
                    value += (
                        physical[0] * flow[index, 3 + c]
                        + physical[1] * flow[index, 6 + c]
                        + physical[2] * flow[index, 9 + c]
                    )
                if c == 0:
                    value += physical[1]
                total[3 * c + index] = value
        in_k = mul(stacked(jnp.concatenate(total, axis=0), 1), z_back[...])
        in_k = jnp.concatenate([in_k[c * NX : (c + 1) * NX] for c in range(9)], axis=1)
        in_m = mul(x_back[...], stacked(in_k, 0))
        for c in range(3):
            outgoing[group, c] = in_m[:, 3 * c * TILE : 3 * (c + 1) * TILE]

        def rows_of(other):
            return pl.ds(pl.multiple_of(other * 8, 8), 8)

        for kind, hop in direct:
            other, device = member(kind, hop)
            send_tiles(
                slot(outgoing, group, everything, rows_of(other)),
                band_of(returned, first_pair, group, everything, everything),
                count == 3,
                back_send.at[group],
                back_recv.at[group],
                device,
            )

        mine = rows_of(place)
        returned[group, :, :, tile_at(first_pair, 2)] = outgoing[
            group, :, mine, pl.ds(0, 2 * TILE)
        ]

        @pl.when(count == 3)
        def _():
            returned[group, :, :, tile_at(first_pair + 2)] = outgoing[
                group, :, mine, pl.ds(2 * TILE, TILE)
            ]

    def finish(group, keep):
        wait_pairs(returned.at[0], back_recv.at[group])
        rows = group_rows(group)
        for pair in range(PAIRS):
            lanes = pl.ds(pair * TILE, TILE)
            value = keep * (fields[rows, :, lanes] + returned[group, :, :, lanes])
            forced[rows, :, lanes] = value
            turned[rows, :, lanes] = pltpu.roll(value, NZ, 2)
        across_heights(
            group, forced, turned, lambda pair, row: solve[pair, row], ends
        )
        if group == 0:
            drain(later, later_recv)
        gap = ends[rows] - later[rows]
        gaps[rows] = gap

        @pl.when(traded)
        def _():
            send(
                gaps.at[rows],
                gaps_home.at[rows],
                home_send.at[group],
                home_recv.at[group],
                trader,
            )

        @pl.when(jnp.logical_not(traded))
        def _():
            gaps_home[rows] = gap

    drain(wall_v, trade_recv.at[0])
    lax.fori_loop(0, PAIRS, solve_rows, 0)
    loads[0].wait()
    begin(0)
    begin(1)
    begin(2)
    shift()
    for load in loads[1:]:
        load.wait()
    keep = kept()
    transform(0)
    transform(1)
    transform(2)
    finish(0, keep)
    finish(1, keep)
    finish(2, keep)

    def products(index, sums):
        lanes = tile_at(index)
        start = [fields[group_rows(g), :, lanes] for g in range(3)]
        gap = [gaps[group_rows(g), :, lanes] for g in range(3)]
        drift = ends[group_rows(0), :, lanes] - start[0]
        terms = [
            drift * start[1],
            drift * start[2],
            gap[1] * gap[1],
            gap[2] * gap[2],
            gap[1] * gap[0],
            gap[2] * gap[0],
            gap[1] * gap[2],
        ]
        return tuple(s + t[0] + t[1] + t[2] for s, t in zip(sums, terms))

    sums = lax.fori_loop(
        0, PAIRS, products, tuple(jnp.zeros((8, TILE), jnp.float32) for _ in range(7))
    )
    column = lax.broadcasted_iota(jnp.int32, (1, TILE), 1)
    message = jnp.zeros((1, TILE), jnp.float32)
    for index, value in enumerate(sums):
        total = jnp.sum(jnp.sum(value, axis=0, keepdims=True), axis=1, keepdims=True)
        message = jnp.where(column == index, total, message)

    def exchange(which, slots, me, size, device, value):
        slots[me] = value
        for step in range(1, size):
            pltpu.make_async_remote_copy(
                src_ref=slots.at[me],
                dst_ref=slots.at[me],
                send_sem=sum_send.at[which],
                recv_sem=sum_recv.at[which],
                device_id=device(step),
                device_id_type=MESH,
            ).start()
        if size > 1:
            drain(slots.at[pl.ds(0, size - 1)], sum_recv.at[which])
        return jnp.sum(slots[...], axis=0)

    slots = [ring_sums, side_sums, far_sums]
    for which, me in enumerate([place, side_me, high]):
        message = exchange(which, slots[which], me, *rounds[which], message)

    def number(index):
        return message[:, index : index + 1]

    root = 1.0 / math.sqrt(nseg * 3 * NX * LANES)
    border = [number(0) * root, number(1) * root]
    diag = [number(2) + border[0] * border[0], number(3) + border[1] * border[1]]
    first = [-number(4) / diag[0], -number(5) / diag[1]]
    cross = number(6) + border[0] * border[1]
    weight = [
        first[0] - first[1] * cross / diag[0],
        first[1] - first[0] * cross / diag[1],
    ]
    weight = [jnp.broadcast_to(value, (8, TILE)) for value in weight]

    @pl.when(traded)
    def _():
        for group in range(3):
            drain(gaps_home.at[group_rows(group)], home_recv.at[group])

    def write(index, carry):
        lanes = tile_at(index)
        for source, target in ((home, corrected), (gaps_home, new_residual)):
            target[0, :, :, lanes] = (
                source[pl.ds(0, 3), :, lanes]
                + weight[0] * source[pl.ds(3, 3), :, lanes]
                + weight[1] * source[pl.ds(6, 3), :, lanes]
            )
        return carry

    lax.fori_loop(0, PAIRS, write, 0)

    for group in range(3):
        wait_pairs(pack.at[:, pl.ds(0, 3)], out_send.at[group])
    for group in range(3):
        @pl.when(count == 3)
        def _():
            drain(outgoing.at[group, :, pl.ds(0, 56), pl.ds(0, 3 * TILE)], back_send.at[group])

        @pl.when(count == 2)
        def _():
            drain(outgoing.at[group, :, pl.ds(0, 56), pl.ds(0, 2 * TILE)], back_send.at[group])

    @pl.when(traded)
    def _():
        for group in range(3):
            drain(fields.at[group_rows(group)], trade_send.at[1 + group])
            drain(gaps.at[group_rows(group)], home_send.at[group])
        drain(wall_v, trade_send.at[0])

    @pl.when(jnp.logical_or(side == 0, core * side == 1))
    def _():
        drain(later, later_send)

    @pl.when(core * (1 - side) == 1)
    def _():
        for group in range(3):
            drain(home.at[group_rows(group)], home_send.at[3 + group])

    for which, (size, _) in enumerate(rounds):
        if size > 1:
            drain(slots[which].at[pl.ds(0, size - 1)], sum_send.at[which])


def local(nseg, constants, states, tangent_panel, wall_inverse, keep_mask):
    operands = (
        states,
        tangent_panel,
        wall_inverse.reshape(8 * NY, NY),
        keep_mask,
        *[jnp.asarray(value) for value in constants],
    )
    f32 = jnp.float32
    sem = pltpu.SemaphoreType.DMA
    whole = (9, 8, LANES)
    scratch = [
        *[pltpu.VMEM(value.shape, value.dtype) for value in constants],
        pltpu.VMEM((8 * NY, NY), f32),
        pltpu.VMEM((NX, NZ), jnp.int32),
        pltpu.VMEM(whole, f32),
        pltpu.VMEM((2, *whole), f32),
        pltpu.VMEM(whole, f32),
        pltpu.VMEM((3, 2, 3, 8, 8, 3 * TILE), f32),
        pltpu.VMEM((3, 12, NX, TILE), f32),
        pltpu.VMEM((3, 3, NX, 3 * TILE), f32),
        pltpu.VMEM((3, 3, 8, LANES), f32),
        pltpu.VMEM((PAIRS, 2 * PAIRS, 8, TILE), f32),
        *[pltpu.VMEM(whole, f32)] * 6,
        pltpu.VMEM((8, 1, TILE), f32),
        pltpu.VMEM((2 * min(4, nseg // 2), 1, TILE), f32),
        pltpu.VMEM((nseg // 2 // min(4, nseg // 2), 1, TILE), f32),
        sem((11,)),
        sem((4,)),
        sem((4,)),
        sem((3,)),
        sem((3,)),
        sem((3,)),
        sem((3,)),
        sem,
        sem,
        sem((6,)),
        sem((3,)),
        sem((3,)),
        sem((3,)),
    ]
    return pl.pallas_call(
        functools.partial(kernel, nseg),
        out_shape=[jax.ShapeDtypeStruct((1, 3, 8, LANES), f32)] * 2,
        in_specs=[pl.BlockSpec(memory_space=pl.ANY)] * len(operands),
        out_specs=[pl.BlockSpec(memory_space=pltpu.VMEM)] * 2,
        scratch_shapes=scratch,
        compiler_params=pltpu.CompilerParams(
            collective_id=0, has_side_effects=True, vmem_limit_bytes=64 * 1024 * 1024
        ),
        name="newton_step",
    )(*operands)


def solution(mesh):
    return jax.shard_map(
        functools.partial(local, mesh.shape["seg"], tables()),
        mesh=mesh,
        in_specs=(
            P("seg", None, "space", None),
            P("seg", None, None, "space", None),
            P("space", None, None),
            P(),
        ),
        out_specs=(P("seg", None, "space", None), P("seg", None, "space", None)),
        check_vma=False,
    )
```
